32 devices in a mesh: space: 16 (over z, x, core), filt: 2 (over y).
Axes of the slice: x: 2, y: 2, z: 4, core: 2. Of those that a mesh axis runs over, the one named last changes fastest.
Arguments:
- activations: bfloat16 [64, 16, 56, 128], P('filt', 'space'), may hold values from -6 to 6
- kernel: bfloat16 [64, 64, 3, 3, 3], P('filt'), may hold values from -0.15625 to 0.15625
- preact: bfloat16 [64, 16, 56, 128], P('filt', 'space'), may hold values from -6 to 6
- upstream: bfloat16 [64, 16, 56, 128], P('filt', 'space'), may hold values from -6 to 6
Outputs:
- input_grad: bfloat16 [64, 16, 56, 128], P('filt', 'space')
- kernel_grad: float32 [64, 64, 3, 3, 3], P('filt')
The draws below stay inside these ranges and needn't reach their ends.
All inputs are finite; a program needn't handle non-finite values.
Results may differ from the reference program's by a relative error of at most 0.0015.
Values may be sent and summed in bfloat16 or wider, within the bound.
A program may use at most 128 MiB of HBM per device.

```python
import jax
import jax.numpy as jnp

CIN = 64
COUT = 64
H = 56
W = 128
NZ = 16


def level_of(key, shape, cuts, low, top_value):
    factor_of = 1.0
    for position, shards_of in cuts:
        draws = jax.random.uniform(jax.random.fold_in(jax.random.fold_in(key, 6), position), (shards_of,), jnp.float32, low / len(cuts), top_value / len(cuts))
        factor_of = factor_of * jnp.repeat(jnp.exp(draws), shape[position] // shards_of).reshape((-1,) + (1,) * (len(shape) - 1 - position))
    return factor_of


def scatter_about(own_key, dims, spread, reach, split=(), dtype=jnp.bfloat16):
    result = spread * jax.random.normal(own_key, dims, jnp.float32)
    if split:
        result = result * level_of(own_key, dims, split, -0.22, 0.18)
    return jnp.clip(result, -reach, reach).astype(dtype)


def setup_inputs(seed: int = 0) -> dict:
    key_list = jax.random.split(jax.random.key(seed), 5)
    return {
        "activations": scatter_about(key_list[0], (CIN, NZ, H, W), 1.0, 6.0, ((0, 2), (1, 16))),
        "kernel": scatter_about(key_list[1], (COUT, CIN, 3, 3, 3), (CIN * 27) ** -0.5, 0.15625, ((0, 2),)),
        "preact": scatter_about(key_list[2], (COUT, NZ, H, W), 1.0, 6.0, ((0, 2), (1, 16))),
        "upstream": scatter_about(key_list[3], (COUT, NZ, H, W), 1.0, 6.0, ((0, 2), (1, 16))),
    }


def data_grad(grad_pad, weight):
    chans = weight.shape[1]
    depth = grad_pad.shape[1] - 2
    rows = grad_pad.shape[2] - 2
    cols = grad_pad.shape[3] - 2
    total = jnp.zeros((chans, depth, rows, cols), jnp.float32)
    for depth_off in range(3):
        for row_off in range(3):
            for col_off in range(3):
                piece = grad_pad[:, 2 - depth_off:2 - depth_off + depth, 2 - row_off:2 - row_off + rows, 2 - col_off:2 - col_off + cols]
                total = total + jnp.einsum('fc,fzyx->czyx', weight[:, :, depth_off, row_off, col_off], piece)
    return total

def weight_grad(grad, input_pad):
    depth, rows, cols = (grad.shape[1], grad.shape[2], grad.shape[3])
    terms = []
    for depth_off in range(3):
        for row_off in range(3):
            for col_off in range(3):
                piece = input_pad[:, depth_off:depth_off + depth, row_off:row_off + rows, col_off:col_off + cols]
                terms.append(jnp.einsum('fzyx,czyx->fc', grad, piece))
    stacked = jnp.stack(terms, axis=-1)
    return stacked.reshape(grad.shape[0], input_pad.shape[0], 3, 3, 3)

def reference(activations, kernel, preact, upstream):
    masked = jnp.where(preact > 0, upstream, jnp.zeros_like(upstream))
    grad32 = masked.astype(jnp.float32)
    input32 = activations.astype(jnp.float32)
    weight32 = kernel.astype(jnp.float32)
    widths = ((0, 0), (1, 1), (1, 1), (1, 1))
    input_grad = data_grad(jnp.pad(grad32, widths), weight32).astype(jnp.bfloat16)
    scale = 1.0 / jnp.sqrt(jnp.float32(NZ * H * W))
    kernel_grad = weight_grad(grad32, jnp.pad(input32, widths)) * scale
    return (input_grad, kernel_grad)
```

```python
import functools

import jax
import jax.numpy as jnp
from jax import lax
from jax.experimental import pallas as pl
from jax.experimental.pallas import tpu as pltpu
from jax.sharding import PartitionSpec as P

MESH = pl.DeviceIdType.MESH
LANES = 128


def kernel_body(
    dims, m_ref, a_ref, k_ref, ig_ref, kg_ref,
    mbuf, abuf, kbuf, ktr, gbuf, rbuf, sbuf, obuf,
    m_recv, sp_send, fl_send, spf_send, flf_send, k_send, k_recv,
    rs_send, rs_recv, ag_send, ag_recv,
):
    S, J, fl, H, R, own, scale = dims
    s = lax.axis_index("space")
    j = lax.axis_index("filt")
    half = (H // 2) * LANES
    cells = H * LANES
    parts = (pl.ds(LANES, half), pl.ds(LANES + half, cells - half))
    k3 = 3 * J * fl

    barrier = pltpu.get_barrier_semaphore()
    count = S * J

    @pl.loop(1, count)
    def _(step):
        other = lax.rem(s * J + j + step, count)
        pl.semaphore_signal(
            barrier, inc=1, device_id={"space": other // J, "filt": lax.rem(other, J)},
            device_id_type=MESH,
        )

    edge = jnp.zeros((3, J, fl, LANES), jnp.bfloat16)
    mbuf[:, :, :, :LANES] = edge
    mbuf[:, :, :, LANES + cells :] = edge
    mbuf[1, j, :, LANES : LANES + cells] = m_ref[...]

    @pl.when(s == 0)
    def _():
        mbuf[0, :, :, LANES : LANES + cells] = jnp.zeros((J, fl, cells), jnp.bfloat16)

    @pl.when(s == S - 1)
    def _():
        mbuf[2, :, :, LANES : LANES + cells] = jnp.zeros((J, fl, cells), jnp.bfloat16)

    pl.semaphore_wait(barrier, count - 1)

    def slab_copy(slot, owner, part, to_slot, space, filt, send):
        return pltpu.make_async_remote_copy(
            src_ref=mbuf.at[slot, owner, :, parts[part]],
            dst_ref=mbuf.at[to_slot, owner, :, parts[part]],
            send_sem=send,
            recv_sem=m_recv.at[to_slot, owner, part],
            device_id={"space": space, "filt": filt},
            device_id_type=MESH,
        )

    def arrived(slot, owner, part):
        ref = mbuf.at[slot, owner, :, parts[part]]
        pltpu.make_async_copy(ref, ref, m_recv.at[slot, owner, part]).wait()

    def valid(d):
        return s > 0 if d < 0 else s < S - 1

    def far(d):
        return lax.rem(s, 2) == (0 if d < 0 else 1)

    def peer(p):
        return lax.rem(j + p, J)

    def k_copy(p):
        return pltpu.make_async_remote_copy(
            src_ref=k_ref.at[peer(p)], dst_ref=kbuf.at[j],
            send_sem=k_send.at[p - 1], recv_sem=k_recv.at[j],
            device_id={"space": s, "filt": peer(p)}, device_id_type=MESH,
        )

    def space_copy(d, part):
        return slab_copy(1, j, part, 1 - d, s + d, j, sp_send.at[(d + 1) // 2, part])

    def filt_copy(p, part):
        return slab_copy(1, j, part, 1, s, peer(p), fl_send.at[p - 1, part])

    def space_forward(d, p, part):
        return slab_copy(
            1, peer(p), part, 1 - d, s + d, j, spf_send.at[(d + 1) // 2, p - 1, part]
        )

    def filt_forward(d, p):
        return slab_copy(1 + d, j, 0, 1 + d, s, peer(p), flf_send.at[(d + 1) // 2, p - 1])

    for first in (0, 1):
        for p in range(1, J):
            filt_copy(p, 1 - first).start()
        for d in (-1, 1):
            @pl.when(valid(d))
            def _():
                space_copy(d, first).start()
    for p in range(1, J):
        k_copy(p).start()

    cl = a_ref.shape[0]
    abuf[...] = jnp.zeros_like(abuf)
    column = lax.broadcasted_iota(jnp.int32, (cl, LANES), 1)

    @pl.loop(0, H)
    def _(row):
        base = pl.multiple_of(row * LANES, LANES)
        x = a_ref[:, pl.ds(base, LANES)].astype(jnp.float32)
        left = jnp.where(column == 0, 0.0, pltpu.roll(x, 1, 1))
        right = jnp.where(column == LANES - 1, 0.0, pltpu.roll(x, LANES - 1, 1))
        to = pl.ds(pl.multiple_of(row * LANES + LANES, LANES), LANES)
        abuf[0:cl, to] = left.astype(jnp.bfloat16)
        abuf[cl : 2 * cl, to] = x.astype(jnp.bfloat16)
        abuf[2 * cl : 3 * cl, to] = right.astype(jnp.bfloat16)

    kbuf[j] = k_ref[j]

    for p in range(1, J):
        arrived(1, peer(p), 1)
        for d in (-1, 1):
            @pl.when(valid(d))
            def _():
                space_forward(d, p, 1).start()
    for d in (-1, 1):
        @pl.when(valid(d))
        def _():
            arrived(1 + d, j, 0)

            @pl.when(far(d))
            def _():
                for p in range(1, J):
                    filt_forward(d, p).start()
    for p in range(1, J):
        arrived(1, peer(p), 0)
        for d in (-1, 1):
            @pl.when(jnp.logical_and(valid(d), jnp.logical_not(far(d))))
            def _():
                space_forward(d, p, 0).start()

    def weight_terms(slot, init):
        if init:
            for q in range(J):
                for dh in range(3):
                    gbuf[q, (dh * 3 + slot) * fl : (dh * 3 + slot + 1) * fl, :] = jnp.zeros(
                        (fl, LANES), jnp.float32
                    )
        rows = 8 if H % 8 == 0 else 1

        @pl.loop(0, H // rows)
        def _(i):
            base = pl.multiple_of(i * rows * LANES, LANES)
            lhs = mbuf[slot, :, :, pl.ds(base + LANES, rows * LANES)].reshape(
                J * fl, rows * LANES
            )
            for dh in range(3):
                rhs = abuf[:, pl.ds(base + dh * LANES, rows * LANES)]
                term = lax.dot_general(
                    lhs, rhs, (((1,), (1,)), ((), ())), preferred_element_type=jnp.float32
                )
                for q in range(J):
                    to = slice((dh * 3 + slot) * fl, (dh * 3 + slot + 1) * fl)
                    gbuf[q, to, :] = gbuf[q, to, :] + term[q * fl : (q + 1) * fl]

    weight_terms(1, True)

    for p in range(1, J):
        got = kbuf.at[peer(p)]
        pltpu.make_async_copy(got, got, k_recv.at[peer(p)]).wait()
    for dh in range(3):
        stacked = jnp.concatenate(
            [kbuf[q, dh, slot] for slot in range(3) for q in range(J)], axis=0
        )
        ktr[dh] = stacked.astype(jnp.float32).T.astype(jnp.bfloat16)

    for d in (-1, 1):
        @pl.when(valid(d))
        def _():
            arrived(1 + d, j, 1)
            for p in range(1, J):
                arrived(1 + d, peer(p), 0)
                arrived(1 + d, peer(p), 1)
        weight_terms(1 + d, True)

    def rs_copy(q, t):
        return pltpu.make_async_remote_copy(
            src_ref=gbuf.at[q, pl.ds(pl.multiple_of(t * R, 8), R)],
            dst_ref=rbuf.at[s, j],
            send_sem=rs_send.at[q, t], recv_sem=rs_recv,
            device_id={"space": t, "filt": q}, device_id_type=MESH,
        )

    def rs_each(act):
        @pl.loop(0, S)
        def _(step):
            t = lax.rem(s + step, S)

            @pl.when(t < own)
            def _():
                for p in range(J):
                    q = peer(p)
                    if p > 0:
                        act(rs_copy(q, t))
                    else:
                        @pl.when(step > 0)
                        def _():
                            act(rs_copy(q, t))

    rs_each(lambda c: c.start())

    @pl.when(s < own)
    def _():
        pltpu.make_async_copy(
            gbuf.at[j, pl.ds(pl.multiple_of(s * R, 8), R)], rbuf.at[s, j], rs_recv
        ).start()

    rows = 4 if H % 4 == 0 else 1
    wide = rows * LANES
    cols = lax.rem(lax.broadcasted_iota(jnp.int32, (cl, wide), 1), LANES)

    @pl.loop(0, H // rows)
    def _(i):
        total = jnp.zeros((3 * cl, wide), jnp.float32)
        for dh in range(3):
            base = pl.multiple_of((i * rows + 2 - dh) * LANES, LANES)
            rhs = mbuf[:, :, :, pl.ds(base, wide)].reshape(k3, wide)
            total = total + jnp.dot(
                ktr[dh, : 3 * cl], rhs, preferred_element_type=jnp.float32
            )
        first = pltpu.roll(total[:cl], wide - 1, 1)
        last = pltpu.roll(total[2 * cl :], 1, 1)
        result = total[cl : 2 * cl] + jnp.where(cols == LANES - 1, 0.0, first)
        result = result + jnp.where(cols == 0, 0.0, last)
        ig_ref[:, pl.ds(pl.multiple_of(i * wide, LANES), wide)] = result.astype(jnp.bfloat16)

    def ag_copy(t):
        return pltpu.make_async_remote_copy(
            src_ref=sbuf, dst_ref=obuf.at[s], send_sem=ag_send.at[t], recv_sem=ag_recv,
            device_id={"space": t, "filt": j}, device_id_type=MESH,
        )

    def ag_each(act):
        @pl.loop(1, S)
        def _(step):
            act(ag_copy(lax.rem(s + step, S)))

    @pl.when(s < own)
    def _():
        pltpu.make_async_copy(rbuf, rbuf, rs_recv).wait()
        total = rbuf[0]
        for t in range(1, S):
            total = total + rbuf[t]
        sbuf[...] = total * scale
        ag_each(lambda c: c.start())
        pltpu.make_async_copy(sbuf, obuf.at[s], ag_recv).start()

    pltpu.make_async_copy(obuf, obuf, ag_recv).wait()
    kg_ref[...] = obuf[...]

    for first in (0, 1):
        for p in range(1, J):
            filt_copy(p, 1 - first).wait_send()
        for d in (-1, 1):
            @pl.when(valid(d))
            def _():
                space_copy(d, first).wait_send()
    for p in range(1, J):
        k_copy(p).wait_send()
        for d in (-1, 1):
            @pl.when(valid(d))
            def _():
                space_forward(d, p, 1).wait_send()

                @pl.when(far(d))
                def _():
                    filt_forward(d, p).wait_send()

                @pl.when(jnp.logical_not(far(d)))
                def _():
                    space_forward(d, p, 0).wait_send()
    rs_each(lambda c: c.wait_send())

    @pl.when(s < own)
    def _():
        ag_each(lambda c: c.wait_send())


def on_device(activations, kernel, preact, upstream):
    S, J = lax.axis_size("space"), lax.axis_size("filt")
    fl, depth, H, W = preact.shape
    cl = activations.shape[0]
    cells = H * W
    volume = S * depth * cells
    scale = 1.0 / float(volume) ** 0.5
    masked = jnp.where(preact > 0, upstream, jnp.zeros_like(upstream)).reshape(fl, cells)
    acts = activations.reshape(cl, cells)
    weights = kernel.reshape(fl, J, cl, 3, 3, 3)[:, :, :, ::-1]
    weights = weights.transpose(1, 4, 3, 0, 5, 2).reshape(J, 3, 3, fl, 3 * cl)
    weights = jnp.pad(weights, ((0, 0),) * 4 + ((0, LANES - 3 * cl),))
    tiles = 9 * fl // 8
    R = 8 * -(-tiles // S)
    own = 9 * fl // R
    dims = (S, J, fl, H, R, own, scale)
    padded = cells + 2 * W
    dma = pltpu.SemaphoreType.DMA
    vmem = pl.BlockSpec(memory_space=pltpu.VMEM)
    peers = max(J - 1, 1)
    ig, kg = pl.pallas_call(
        functools.partial(kernel_body, dims),
        out_shape=(
            jax.ShapeDtypeStruct((cl, cells), jnp.bfloat16),
            jax.ShapeDtypeStruct((own, J, R, LANES), jnp.float32),
        ),
        in_specs=[vmem] * 3,
        out_specs=(vmem, vmem),
        scratch_shapes=[
            pltpu.VMEM((3, J, fl, padded), jnp.bfloat16),
            pltpu.VMEM((LANES, padded), jnp.bfloat16),
            pltpu.VMEM((J, 3, 3, fl, LANES), jnp.bfloat16),
            pltpu.VMEM((3, LANES, 3 * J * fl), jnp.bfloat16),
            pltpu.VMEM((J, 9 * fl, LANES), jnp.float32),
            pltpu.VMEM((S, J, R, LANES), jnp.float32),
            pltpu.VMEM((J, R, LANES), jnp.float32),
            pltpu.VMEM((own, J, R, LANES), jnp.float32),
            dma((3, J, 2)), dma((2, 2)), dma((peers, 2)), dma((2, peers, 2)),
            dma((2, peers)), dma((peers,)), dma((J,)),
            dma((J, own)), dma, dma((S,)), dma,
        ],
        compiler_params=pltpu.CompilerParams(
            collective_id=0, has_side_effects=True, vmem_limit_bytes=40 * 2**20
        ),
    )(masked, acts, weights)
    input_grad = ig.reshape(cl, depth, H, W)
    kg = kg.transpose(0, 2, 1, 3).reshape(3, 3, fl, J, LANES)[:, ::-1, :, :, : 3 * cl]
    kg = kg.reshape(3, 3, fl, J, 3, cl).transpose(2, 3, 5, 1, 0, 4)
    return (input_grad, kg.reshape(fl, J * cl, 3, 3, 3))


def solution(mesh):
    in_specs = (
        P("filt", "space", None, None),
        P("filt", None, None, None, None),
        P("filt", "space", None, None),
        P("filt", "space", None, None),
    )
    out_specs = (P("filt", "space", None, None), P("filt", None, None, None, None))
    return jax.shard_map(
        on_device, mesh=mesh, in_specs=in_specs, out_specs=out_specs, check_vma=False
    )
```

```python
import functools

import jax
import jax.numpy as jnp
from jax import lax
from jax.experimental import pallas as pl
from jax.experimental.pallas import tpu as pltpu
from jax.sharding import PartitionSpec as P

MESH = pl.DeviceIdType.MESH
LANES = 128


def kernel_body(
    dims, m_ref, a_ref, k_ref, ig_ref, kg_ref,
    mbuf, abuf, kbuf, ktr, gbuf, pbuf, hbuf, rbuf, sbuf, obuf,
    m_recv, sp_send, fl_send, spf_send, flf_send, k_send, k_recv,
    pair_send, pair_recv, rs_send, rs_recv, ag_send, ag_recv, sib_send, sib_recv,
):
    S, J, fl, H, R, owners, scale = dims
    s = lax.axis_index("space")
    j = lax.axis_index("filt")
    core = lax.rem(s, 2)
    chip = s // 2
    chips = S // 2
    sibling = s + 1 - 2 * core
    keep = R * owners
    mine = (chip * owners + chips - 1) // chips
    is_owner = jnp.logical_and(mine < owners, (mine * chips) // owners == chip)
    half = (H // 2) * LANES
    cells = H * LANES
    parts = (pl.ds(LANES, half), pl.ds(LANES + half, cells - half))
    k3 = 3 * J * fl
    cl = a_ref.shape[0]

    def valid(d):
        return s > 0 if d < 0 else s < S - 1

    def far(d):
        return core == (0 if d < 0 else 1)

    def peer(p):
        return lax.rem(j + p, J)

    barrier = pltpu.get_barrier_semaphore()
    for d in (-1, 1):
        @pl.when(valid(d))
        def _():
            pl.semaphore_signal(
                barrier, inc=1, device_id={"space": s + d, "filt": j}, device_id_type=MESH
            )

    @pl.loop(1, chips * J)
    def _(step):
        other = lax.rem(chip * J + j + step, chips * J)
        pl.semaphore_signal(
            barrier, inc=1,
            device_id={"space": 2 * (other // J) + core, "filt": lax.rem(other, J)},
            device_id_type=MESH,
        )

    edge = jnp.zeros((3, J, fl, LANES), jnp.bfloat16)
    mbuf[:, :, :, :LANES] = edge
    mbuf[:, :, :, LANES + cells :] = edge
    mbuf[1, j, :, LANES : LANES + cells] = m_ref[...]

    @pl.when(s == 0)
    def _():
        mbuf[0, :, :, LANES : LANES + cells] = jnp.zeros((J, fl, cells), jnp.bfloat16)

    @pl.when(s == S - 1)
    def _():
        mbuf[2, :, :, LANES : LANES + cells] = jnp.zeros((J, fl, cells), jnp.bfloat16)

    next_to = (s > 0).astype(jnp.int32) + (s < S - 1).astype(jnp.int32)
    pl.semaphore_wait(barrier, chips * J - 1 + next_to)

    def slab_copy(slot, owner, part, to_slot, space, filt, send):
        return pltpu.make_async_remote_copy(
            src_ref=mbuf.at[slot, owner, :, parts[part]],
            dst_ref=mbuf.at[to_slot, owner, :, parts[part]],
            send_sem=send,
            recv_sem=m_recv.at[to_slot, owner, part],
            device_id={"space": space, "filt": filt},
            device_id_type=MESH,
        )

    def arrived(slot, owner, part):
        ref = mbuf.at[slot, owner, :, parts[part]]
        pltpu.make_async_copy(ref, ref, m_recv.at[slot, owner, part]).wait()

    def k_copy(p):
        return pltpu.make_async_remote_copy(
            src_ref=k_ref.at[peer(p)], dst_ref=kbuf.at[j],
            send_sem=k_send.at[p - 1], recv_sem=k_recv.at[j],
            device_id={"space": s, "filt": peer(p)}, device_id_type=MESH,
        )

    def space_copy(d, part):
        return slab_copy(1, j, part, 1 - d, s + d, j, sp_send.at[(d + 1) // 2, part])

    def filt_copy(p, part):
        return slab_copy(1, j, part, 1, s, peer(p), fl_send.at[p - 1, part])

    def space_forward(d, p, part):
        return slab_copy(
            1, peer(p), part, 1 - d, s + d, j, spf_send.at[(d + 1) // 2, p - 1, part]
        )

    def filt_forward(d, p):
        return slab_copy(1 + d, j, 0, 1 + d, s, peer(p), flf_send.at[(d + 1) // 2, p - 1])

    for first in (0, 1):
        for p in range(1, J):
            filt_copy(p, 1 - first).start()
        for d in (-1, 1):
            @pl.when(valid(d))
            def _():
                space_copy(d, first).start()
    for p in range(1, J):
        k_copy(p).start()

    abuf[...] = jnp.zeros_like(abuf)
    gbuf[...] = jnp.zeros_like(gbuf)
    kbuf[j] = k_ref[j]
    column = lax.broadcasted_iota(jnp.int32, (cl, LANES), 1)

    @pl.loop(0, H)
    def _(row):
        base = pl.multiple_of(row * LANES, LANES)
        x = a_ref[:, pl.ds(base, LANES)].astype(jnp.float32)
        left = jnp.where(column == 0, 0.0, pltpu.roll(x, 1, 1))
        right = jnp.where(column == LANES - 1, 0.0, pltpu.roll(x, LANES - 1, 1))
        to = pl.ds(pl.multiple_of(row * LANES + LANES, LANES), LANES)
        abuf[0:cl, to] = left.astype(jnp.bfloat16)
        abuf[cl : 2 * cl, to] = x.astype(jnp.bfloat16)
        abuf[2 * cl : 3 * cl, to] = right.astype(jnp.bfloat16)

    def weight_terms(pieces, part):
        rows = H // 4

        @pl.loop(2 * part, 2 * part + 2)
        def _(i):
            base = pl.multiple_of(i * rows * LANES, LANES)
            lhs = jnp.concatenate(
                [mbuf[slot, q, :, pl.ds(base + LANES, rows * LANES)] for slot, q in pieces],
                axis=0,
            )
            for dh in range(3):
                rhs = abuf[:, pl.ds(base + dh * LANES, rows * LANES)]
                term = lax.dot_general(
                    lhs, rhs, (((1,), (1,)), ((), ())), preferred_element_type=jnp.float32
                )
                for n, (slot, q) in enumerate(pieces):
                    to = slice((dh * 3 + slot) * fl, (dh * 3 + slot + 1) * fl)
                    gbuf[q, to, :] = gbuf[q, to, :] + term[n * fl : (n + 1) * fl]

    centre = [(1, q) for q in range(J)]
    own_next = [(0, j), (2, j)]
    other_next = [(slot, peer(p)) for p in range(1, J) for slot in (0, 2)]

    for p in range(1, J):
        arrived(1, peer(p), 1)
        for d in (-1, 1):
            @pl.when(valid(d))
            def _():
                space_forward(d, p, 1).start()
    for d in (-1, 1):
        @pl.when(valid(d))
        def _():
            arrived(1 + d, j, 0)

            @pl.when(far(d))
            def _():
                for p in range(1, J):
                    filt_forward(d, p).start()
    weight_terms(centre, 1)
    weight_terms(own_next, 0)
    for p in range(1, J):
        arrived(1, peer(p), 0)
        for d in (-1, 1):
            @pl.when(jnp.logical_and(valid(d), jnp.logical_not(far(d))))
            def _():
                space_forward(d, p, 0).start()
    weight_terms(centre, 0)
    for d in (-1, 1):
        @pl.when(valid(d))
        def _():
            arrived(1 + d, j, 1)
    weight_terms(own_next, 1)

    for p in range(1, J):
        got = kbuf.at[peer(p)]
        pltpu.make_async_copy(got, got, k_recv.at[peer(p)]).wait()
    for dh in range(3):
        stacked = jnp.concatenate(
            [kbuf[q, dh, slot] for slot in range(3) for q in range(J)], axis=0
        )
        ktr[dh] = stacked.astype(jnp.float32).T.astype(jnp.bfloat16)

    for part in (1, 0):
        for d in (-1, 1):
            @pl.when(valid(d))
            def _():
                for p in range(1, J):
                    arrived(1 + d, peer(p), part)
        if J > 1:
            weight_terms(other_next, part)

    def pair_copy():
        return pltpu.make_async_remote_copy(
            src_ref=gbuf.at[:, pl.ds(pl.multiple_of((1 - core) * keep, 8), keep)],
            dst_ref=pbuf, send_sem=pair_send, recv_sem=pair_recv,
            device_id={"space": sibling, "filt": j}, device_id_type=MESH,
        )

    def rs_copy(q, o):
        return pltpu.make_async_remote_copy(
            src_ref=hbuf.at[q, pl.ds(pl.multiple_of(o * R, 8), R)],
            dst_ref=rbuf.at[chip, j],
            send_sem=rs_send.at[q, o], recv_sem=rs_recv,
            device_id={"space": 2 * ((o * chips) // owners) + core, "filt": q},
            device_id_type=MESH,
        )

    def rs_each(act):
        @pl.loop(0, owners)
        def _(step):
            o = lax.rem(mine + step, owners)
            for p in range(J):
                q = peer(p)
                if p > 0:
                    act(rs_copy(q, o))
                else:
                    @pl.when((o * chips) // owners != chip)
                    def _():
                        act(rs_copy(q, o))

    def ag_copy(t):
        return pltpu.make_async_remote_copy(
            src_ref=sbuf, dst_ref=obuf.at[core, mine], send_sem=ag_send.at[t],
            recv_sem=ag_recv,
            device_id={"space": 2 * t + core, "filt": j}, device_id_type=MESH,
        )

    def ag_each(act):
        @pl.loop(1, chips)
        def _(step):
            act(ag_copy(lax.rem(chip + step, chips)))

    def sib_copy():
        return pltpu.make_async_remote_copy(
            src_ref=obuf.at[core], dst_ref=obuf.at[core],
            send_sem=sib_send, recv_sem=sib_recv,
            device_id={"space": sibling, "filt": j}, device_id_type=MESH,
        )

    rows = H // 8
    wide = rows * LANES
    cols = lax.rem(lax.broadcasted_iota(jnp.int32, (cl, wide), 1), LANES)

    def input_part(first_step, last_step):
        @pl.loop(first_step, last_step)
        def _(i):
            for sub in range(2):
                at = (2 * i + sub) * rows
                total = jnp.zeros((3 * cl, wide), jnp.float32)
                for dh in range(3):
                    base = pl.multiple_of((at + 2 - dh) * LANES, LANES)
                    rhs = mbuf[:, :, :, pl.ds(base, wide)].reshape(k3, wide)
                    total = total + jnp.dot(
                        ktr[dh, : 3 * cl], rhs, preferred_element_type=jnp.float32
                    )
                first = pltpu.roll(total[:cl], wide - 1, 1)
                last = pltpu.roll(total[2 * cl :], 1, 1)
                result = total[cl : 2 * cl] + jnp.where(cols == LANES - 1, 0.0, first)
                result = result + jnp.where(cols == 0, 0.0, last)
                to = pl.ds(pl.multiple_of(at * LANES, LANES), wide)
                ig_ref[:, to] = result.astype(jnp.bfloat16)

    pair_copy().start()
    input_part(0, 1)
    pair_copy().wait_recv()
    hbuf[...] = gbuf[:, pl.ds(pl.multiple_of(core * keep, 8), keep)] + pbuf[...]
    rs_each(lambda c: c.start())

    @pl.when(is_owner)
    def _():
        pltpu.make_async_copy(
            hbuf.at[j, pl.ds(pl.multiple_of(mine * R, 8), R)], rbuf.at[chip, j], rs_recv
        ).start()

    input_part(1, 3)

    @pl.when(is_owner)
    def _():
        pltpu.make_async_copy(rbuf, rbuf, rs_recv).wait()
        total = rbuf[0]
        for t in range(1, chips):
            total = total + rbuf[t]
        sbuf[...] = total * scale
        ag_each(lambda c: c.start())
        pltpu.make_async_copy(sbuf, obuf.at[core, mine], ag_recv).start()

    input_part(3, 4)
    pltpu.make_async_copy(obuf.at[core], obuf.at[core], ag_recv).wait()
    sib_copy().start()
    kg_ref[core] = obuf[core]
    sib_copy().wait_recv()
    kg_ref[1 - core] = obuf[1 - core]

    for first in (0, 1):
        for p in range(1, J):
            filt_copy(p, 1 - first).wait_send()
        for d in (-1, 1):
            @pl.when(valid(d))
            def _():
                space_copy(d, first).wait_send()
    for p in range(1, J):
        k_copy(p).wait_send()
        for d in (-1, 1):
            @pl.when(valid(d))
            def _():
                space_forward(d, p, 1).wait_send()

                @pl.when(far(d))
                def _():
                    filt_forward(d, p).wait_send()

                @pl.when(jnp.logical_not(far(d)))
                def _():
                    space_forward(d, p, 0).wait_send()
    pair_copy().wait_send()
    rs_each(lambda c: c.wait_send())

    @pl.when(is_owner)
    def _():
        ag_each(lambda c: c.wait_send())

    sib_copy().wait_send()


def on_device(activations, kernel, preact, upstream):
    S, J = lax.axis_size("space"), lax.axis_size("filt")
    fl, depth, H, W = preact.shape
    cl = activations.shape[0]
    cells = H * W
    volume = S * depth * cells
    scale = 1.0 / float(volume) ** 0.5
    masked = jnp.where(preact > 0, upstream, jnp.zeros_like(upstream)).reshape(fl, cells)
    acts = activations.reshape(cl, cells)
    weights = kernel.reshape(fl, J, cl, 3, 3, 3)[:, :, :, ::-1]
    weights = weights.transpose(1, 4, 3, 0, 5, 2).reshape(J, 3, 3, fl, 3 * cl)
    weights = jnp.pad(weights, ((0, 0),) * 4 + ((0, LANES - 3 * cl),))
    chips = S // 2
    tiles = -(-9 * fl // 16)
    R = 8 * -(-tiles // chips)
    owners = -(-8 * tiles // R)
    keep = R * owners
    dims = (S, J, fl, H, R, owners, scale)
    padded = cells + 2 * W
    dma = pltpu.SemaphoreType.DMA
    vmem = pl.BlockSpec(memory_space=pltpu.VMEM)
    peers = max(J - 1, 1)
    ig, kg = pl.pallas_call(
        functools.partial(kernel_body, dims),
        out_shape=(
            jax.ShapeDtypeStruct((cl, cells), jnp.bfloat16),
            jax.ShapeDtypeStruct((2, owners, J, R, LANES), jnp.float32),
        ),
        in_specs=[vmem] * 3,
        out_specs=(vmem, vmem),
        scratch_shapes=[
            pltpu.VMEM((3, J, fl, padded), jnp.bfloat16),
            pltpu.VMEM((LANES, padded), jnp.bfloat16),
            pltpu.VMEM((J, 3, 3, fl, LANES), jnp.bfloat16),
            pltpu.VMEM((3, LANES, 3 * J * fl), jnp.bfloat16),
            pltpu.VMEM((J, 2 * keep, LANES), jnp.float32),
            pltpu.VMEM((J, keep, LANES), jnp.float32),
            pltpu.VMEM((J, keep, LANES), jnp.float32),
            pltpu.VMEM((chips, J, R, LANES), jnp.float32),
            pltpu.VMEM((J, R, LANES), jnp.float32),
            pltpu.VMEM((2, owners, J, R, LANES), jnp.float32),
            dma((3, J, 2)), dma((2, 2)), dma((peers, 2)), dma((2, peers, 2)),
            dma((2, peers)), dma((peers,)), dma((J,)),
            dma, dma, dma((J, owners)), dma, dma((chips,)), dma, dma, dma,
        ],
        compiler_params=pltpu.CompilerParams(
            collective_id=0, has_side_effects=True, vmem_limit_bytes=40 * 2**20
        ),
    )(masked, acts, weights)
    input_grad = ig.reshape(cl, depth, H, W)
    kg = kg.transpose(0, 1, 3, 2, 4).reshape(2 * keep, J, LANES)[: 9 * fl]
    kg = kg.reshape(3, 3, fl, J, LANES)[:, ::-1, :, :, : 3 * cl]
    kg = kg.reshape(3, 3, fl, J, 3, cl).transpose(2, 3, 5, 1, 0, 4)
    return (input_grad, kg.reshape(fl, J * cl, 3, 3, 3))


def solution(mesh):
    in_specs = (
        P("filt", "space", None, None),
        P("filt", None, None, None, None),
        P("filt", "space", None, None),
        P("filt", "space", None, None),
    )
    out_specs = (P("filt", "space", None, None), P("filt", None, None, None, None))
    return jax.shard_map(
        on_device, mesh=mesh, in_specs=in_specs, out_specs=out_specs, check_vma=False
    )
```

```python
import functools

import jax
import jax.numpy as jnp
from jax import lax
from jax.experimental import pallas as pl
from jax.experimental.pallas import tpu as pltpu
from jax.sharding import PartitionSpec as P

MESH = pl.DeviceIdType.MESH
LANES = 128


def kernel_body(
    dims, m_ref, a_ref, k_ref, ig_ref, kg_ref,
    mbuf, abuf, kpart, kbuf, ktr, gbuf, pbuf, hbuf, rbuf, sbuf, obuf,
    m_recv, sp_send, fl_send, spf_send, flf_send, k_send, k_recv,
    pair_send, pair_recv, rs_send, rs_recv, ag_send, ag_recv, sib_send, sib_recv,
):
    S, J, fl, H, R, owners, scale = dims
    s = lax.axis_index("space")
    j = lax.axis_index("filt")
    core = lax.rem(s, 2)
    chip = s // 2
    chips = S // 2
    sibling = s + 1 - 2 * core
    keep = R * owners
    mine = (chip * owners + chips - 1) // chips
    is_owner = jnp.logical_and(mine < owners, (mine * chips) // owners == chip)
    half = (H // 2) * LANES
    cells = H * LANES
    parts = (pl.ds(LANES, half), pl.ds(LANES + half, cells - half))
    k3 = 3 * J * fl
    cl = a_ref.shape[0]

    def valid(d):
        return s > 0 if d < 0 else s < S - 1

    def far(d):
        return core == (0 if d < 0 else 1)

    def peer(p):
        return lax.rem(j + p, J)

    barrier = pltpu.get_barrier_semaphore()
    for d in (-1, 1):
        @pl.when(valid(d))
        def _():
            pl.semaphore_signal(
                barrier, inc=1, device_id={"space": s + d, "filt": j}, device_id_type=MESH
            )

    @pl.loop(1, chips * J)
    def _(step):
        other = lax.rem(chip * J + j + step, chips * J)
        pl.semaphore_signal(
            barrier, inc=1,
            device_id={"space": 2 * (other // J) + core, "filt": lax.rem(other, J)},
            device_id_type=MESH,
        )

    edge = jnp.zeros((3, J, fl, LANES), jnp.bfloat16)
    mbuf[:, :, :, :LANES] = edge
    mbuf[:, :, :, LANES + cells :] = edge
    mbuf[1, j, :, LANES : LANES + cells] = m_ref[...]

    @pl.when(s == 0)
    def _():
        mbuf[0, :, :, LANES : LANES + cells] = jnp.zeros((J, fl, cells), jnp.bfloat16)

    @pl.when(s == S - 1)
    def _():
        mbuf[2, :, :, LANES : LANES + cells] = jnp.zeros((J, fl, cells), jnp.bfloat16)

    next_to = (s > 0).astype(jnp.int32) + (s < S - 1).astype(jnp.int32)
    pl.semaphore_wait(barrier, chips * J - 1 + next_to)

    def slab_copy(slot, owner, part, to_slot, space, filt, send):
        return pltpu.make_async_remote_copy(
            src_ref=mbuf.at[slot, owner, :, parts[part]],
            dst_ref=mbuf.at[to_slot, owner, :, parts[part]],
            send_sem=send,
            recv_sem=m_recv.at[to_slot, owner, part],
            device_id={"space": space, "filt": filt},
            device_id_type=MESH,
        )

    def arrived(slot, owner, part):
        ref = mbuf.at[slot, owner, :, parts[part]]
        pltpu.make_async_copy(ref, ref, m_recv.at[slot, owner, part]).wait()

    def k_copy(p):
        return pltpu.make_async_remote_copy(
            src_ref=kpart.at[peer(p)], dst_ref=kbuf.at[j],
            send_sem=k_send.at[p - 1], recv_sem=k_recv.at[j],
            device_id={"space": s, "filt": peer(p)}, device_id_type=MESH,
        )

    def space_copy(d, part):
        return slab_copy(1, j, part, 1 - d, s + d, j, sp_send.at[(d + 1) // 2, part])

    def filt_copy(p, part):
        return slab_copy(1, j, part, 1, s, peer(p), fl_send.at[p - 1, part])

    def space_forward(d, p, part):
        return slab_copy(
            1, peer(p), part, 1 - d, s + d, j, spf_send.at[(d + 1) // 2, p - 1, part]
        )

    def filt_forward(d, p):
        return slab_copy(1 + d, j, 0, 1 + d, s, peer(p), flf_send.at[(d + 1) // 2, p - 1])

    for first in (0, 1):
        for p in range(1, J):
            filt_copy(p, 1 - first).start()
        for d in (-1, 1):
            @pl.when(valid(d))
            def _():
                space_copy(d, first).start()

    abuf[:LANES] = jnp.zeros((LANES, LANES), jnp.bfloat16)
    abuf[LANES + cells :] = jnp.zeros((LANES, LANES), jnp.bfloat16)
    gbuf[...] = jnp.zeros_like(gbuf)
    column = lax.broadcasted_iota(jnp.int32, (cl, LANES), 1)

    @pl.loop(0, H)
    def _(row):
        base = pl.multiple_of(row * LANES, LANES)
        x = a_ref[:, pl.ds(base, LANES)].astype(jnp.float32)
        left = jnp.where(column == 0, 0.0, pltpu.roll(x, 1, 1))
        right = jnp.where(column == LANES - 1, 0.0, pltpu.roll(x, LANES - 1, 1))
        rest = jnp.zeros((LANES - 3 * cl, LANES), jnp.float32)
        stacked = jnp.concatenate([left, x, right, rest], axis=0)
        to = pl.ds(pl.multiple_of(row * LANES + LANES, LANES), LANES)
        abuf[to, :] = stacked.T.astype(jnp.bfloat16)

    for q in range(J):
        for dh in range(3):
            for slot in range(3):
                taps = [
                    k_ref[(2 - slot) * 9 + dh * 3 + dw].astype(jnp.float32)[
                        :, q * cl : (q + 1) * cl
                    ]
                    for dw in range(3)
                ]
                taps.append(jnp.zeros((fl, LANES - 3 * cl), jnp.float32))
                kpart[q, dh, slot] = jnp.concatenate(taps, axis=1).astype(jnp.bfloat16)
    for p in range(1, J):
        k_copy(p).start()
    kbuf[j] = kpart[j]

    def weight_terms(pieces, part):
        rows = H // 4

        @pl.loop(2 * part, 2 * part + 2)
        def _(i):
            base = pl.multiple_of(i * rows * LANES, LANES)
            lhs = jnp.concatenate(
                [mbuf[slot, q, :, pl.ds(base + LANES, rows * LANES)] for slot, q in pieces],
                axis=0,
            )
            rhs = jnp.concatenate(
                [abuf[pl.ds(base + dh * LANES, rows * LANES), :] for dh in range(3)], axis=1
            )
            term = jnp.dot(lhs, rhs, preferred_element_type=jnp.float32)
            for dh in range(3):
                for n, (slot, q) in enumerate(pieces):
                    to = slice((dh * 3 + slot) * fl, (dh * 3 + slot + 1) * fl)
                    gbuf[q, to, :] = gbuf[q, to, :] + term[
                        n * fl : (n + 1) * fl, dh * LANES : (dh + 1) * LANES
                    ]

    centre = [(1, q) for q in range(J)]
    own_next = [(0, j), (2, j)]
    other_next = [(slot, peer(p)) for p in range(1, J) for slot in (0, 2)]

    for p in range(1, J):
        arrived(1, peer(p), 1)
        for d in (-1, 1):
            @pl.when(valid(d))
            def _():
                space_forward(d, p, 1).start()
    for d in (-1, 1):
        @pl.when(valid(d))
        def _():
            arrived(1 + d, j, 0)

            @pl.when(far(d))
            def _():
                for p in range(1, J):
                    filt_forward(d, p).start()
    weight_terms(centre, 1)
    weight_terms(own_next, 0)
    for p in range(1, J):
        arrived(1, peer(p), 0)
        for d in (-1, 1):
            @pl.when(jnp.logical_and(valid(d), jnp.logical_not(far(d))))
            def _():
                space_forward(d, p, 0).start()
    weight_terms(centre, 0)
    for d in (-1, 1):
        @pl.when(valid(d))
        def _():
            arrived(1 + d, j, 1)
    weight_terms(own_next, 1)

    for p in range(1, J):
        got = kbuf.at[peer(p)]
        pltpu.make_async_copy(got, got, k_recv.at[peer(p)]).wait()
    for dh in range(3):
        stacked = jnp.concatenate(
            [kbuf[q, dh, slot] for slot in range(3) for q in range(J)], axis=0
        )
        ktr[dh] = stacked.astype(jnp.float32).T.astype(jnp.bfloat16)

    for part in (1, 0):
        for d in (-1, 1):
            @pl.when(valid(d))
            def _():
                for p in range(1, J):
                    arrived(1 + d, peer(p), part)
        if J > 1:
            weight_terms(other_next, part)

    def pair_copy():
        return pltpu.make_async_remote_copy(
            src_ref=gbuf.at[:, pl.ds(pl.multiple_of((1 - core) * keep, 8), keep)],
            dst_ref=pbuf, send_sem=pair_send, recv_sem=pair_recv,
            device_id={"space": sibling, "filt": j}, device_id_type=MESH,
        )

    def rs_copy(q, o):
        return pltpu.make_async_remote_copy(
            src_ref=hbuf.at[q, pl.ds(pl.multiple_of(o * R, 8), R)],
            dst_ref=rbuf.at[chip, j],
            send_sem=rs_send.at[q, o], recv_sem=rs_recv,
            device_id={"space": 2 * ((o * chips) // owners) + core, "filt": q},
            device_id_type=MESH,
        )

    def rs_each(act):
        @pl.loop(0, owners)
        def _(step):
            o = lax.rem(mine + step, owners)
            for p in range(J):
                q = peer(p)
                if p > 0:
                    act(rs_copy(q, o))
                else:
                    @pl.when((o * chips) // owners != chip)
                    def _():
                        act(rs_copy(q, o))

    def ag_copy(t):
        return pltpu.make_async_remote_copy(
            src_ref=sbuf, dst_ref=obuf.at[core, mine], send_sem=ag_send.at[t],
            recv_sem=ag_recv,
            device_id={"space": 2 * t + core, "filt": j}, device_id_type=MESH,
        )

    def ag_each(act):
        @pl.loop(1, chips)
        def _(step):
            act(ag_copy(lax.rem(chip + step, chips)))

    def sib_copy():
        return pltpu.make_async_remote_copy(
            src_ref=obuf.at[core], dst_ref=obuf.at[core],
            send_sem=sib_send, recv_sem=sib_recv,
            device_id={"space": sibling, "filt": j}, device_id_type=MESH,
        )

    rows = H // 8
    wide = rows * LANES
    cols = lax.rem(lax.broadcasted_iota(jnp.int32, (cl, wide), 1), LANES)

    def input_part(first_step, last_step):
        @pl.loop(first_step, last_step)
        def _(i):
            for sub in range(2):
                at = (2 * i + sub) * rows
                total = jnp.zeros((3 * cl, wide), jnp.float32)
                for dh in range(3):
                    base = pl.multiple_of((at + 2 - dh) * LANES, LANES)
                    rhs = mbuf[:, :, :, pl.ds(base, wide)].reshape(k3, wide)
                    total = total + jnp.dot(
                        ktr[dh, : 3 * cl], rhs, preferred_element_type=jnp.float32
                    )
                first = pltpu.roll(total[:cl], wide - 1, 1)
                last = pltpu.roll(total[2 * cl :], 1, 1)
                result = total[cl : 2 * cl] + jnp.where(cols == LANES - 1, 0.0, first)
                result = result + jnp.where(cols == 0, 0.0, last)
                to = pl.ds(pl.multiple_of(at * LANES, LANES), wide)
                ig_ref[:, to] = result.astype(jnp.bfloat16)

    pair_copy().start()
    input_part(0, 1)
    pair_copy().wait_recv()
    hbuf[...] = gbuf[:, pl.ds(pl.multiple_of(core * keep, 8), keep)] + pbuf[...]
    rs_each(lambda c: c.start())

    @pl.when(is_owner)
    def _():
        pltpu.make_async_copy(
            hbuf.at[j, pl.ds(pl.multiple_of(mine * R, 8), R)], rbuf.at[chip, j], rs_recv
        ).start()

    input_part(1, 3)

    @pl.when(is_owner)
    def _():
        pltpu.make_async_copy(rbuf, rbuf, rs_recv).wait()
        total = rbuf[0]
        for t in range(1, chips):
            total = total + rbuf[t]
        sbuf[...] = total * scale
        ag_each(lambda c: c.start())
        pltpu.make_async_copy(sbuf, obuf.at[core, mine], ag_recv).start()

    input_part(3, 4)
    pltpu.make_async_copy(obuf.at[core], obuf.at[core], ag_recv).wait()
    sib_copy().start()
    sib_copy().wait_recv()
    blocks = [obuf[:, :, q].reshape(2 * keep, LANES) for q in range(J)]
    for dh in range(3):
        for slot in range(3):
            at = (dh * 3 + slot) * fl
            for dw in range(3):
                kg_ref[(2 - slot) * 9 + dh * 3 + dw] = jnp.concatenate(
                    [b[at : at + fl, dw * cl : (dw + 1) * cl] for b in blocks], axis=1
                )

    for first in (0, 1):
        for p in range(1, J):
            filt_copy(p, 1 - first).wait_send()
        for d in (-1, 1):
            @pl.when(valid(d))
            def _():
                space_copy(d, first).wait_send()
    for p in range(1, J):
        k_copy(p).wait_send()
        for d in (-1, 1):
            @pl.when(valid(d))
            def _():
                space_forward(d, p, 1).wait_send()

                @pl.when(far(d))
                def _():
                    filt_forward(d, p).wait_send()

                @pl.when(jnp.logical_not(far(d)))
                def _():
                    space_forward(d, p, 0).wait_send()
    pair_copy().wait_send()
    rs_each(lambda c: c.wait_send())

    @pl.when(is_owner)
    def _():
        ag_each(lambda c: c.wait_send())

    sib_copy().wait_send()


def on_device(activations, kernel, preact, upstream):
    S, J = lax.axis_size("space"), lax.axis_size("filt")
    fl, depth, H, W = preact.shape
    cl = activations.shape[0]
    cells = H * W
    volume = S * depth * cells
    scale = 1.0 / float(volume) ** 0.5
    masked = jnp.where(preact > 0, upstream, jnp.zeros_like(upstream)).reshape(fl, cells)
    acts = activations.reshape(cl, cells)
    taps = kernel.transpose(2, 3, 4, 0, 1).reshape(27, fl, J * cl)
    chips = S // 2
    tiles = -(-9 * fl // 16)
    R = 8 * -(-tiles // chips)
    owners = -(-8 * tiles // R)
    keep = R * owners
    dims = (S, J, fl, H, R, owners, scale)
    padded = cells + 2 * W
    dma = pltpu.SemaphoreType.DMA
    vmem = pl.BlockSpec(memory_space=pltpu.VMEM)
    peers = max(J - 1, 1)
    ig, kg = pl.pallas_call(
        functools.partial(kernel_body, dims),
        out_shape=(
            jax.ShapeDtypeStruct((cl, cells), jnp.bfloat16),
            jax.ShapeDtypeStruct((27, fl, J * cl), jnp.float32),
        ),
        in_specs=[vmem] * 3,
        out_specs=(vmem, vmem),
        scratch_shapes=[
            pltpu.VMEM((3, J, fl, padded), jnp.bfloat16),
            pltpu.VMEM((padded, LANES), jnp.bfloat16),
            pltpu.VMEM((J, 3, 3, fl, LANES), jnp.bfloat16),
            pltpu.VMEM((J, 3, 3, fl, LANES), jnp.bfloat16),
            pltpu.VMEM((3, LANES, 3 * J * fl), jnp.bfloat16),
            pltpu.VMEM((J, 2 * keep, LANES), jnp.float32),
            pltpu.VMEM((J, keep, LANES), jnp.float32),
            pltpu.VMEM((J, keep, LANES), jnp.float32),
            pltpu.VMEM((chips, J, R, LANES), jnp.float32),
            pltpu.VMEM((J, R, LANES), jnp.float32),
            pltpu.VMEM((2, owners, J, R, LANES), jnp.float32),
            dma((3, J, 2)), dma((2, 2)), dma((peers, 2)), dma((2, peers, 2)),
            dma((2, peers)), dma((peers,)), dma((J,)),
            dma, dma, dma((J, owners)), dma, dma((chips,)), dma, dma, dma,
        ],
        compiler_params=pltpu.CompilerParams(
            collective_id=0, has_side_effects=True, vmem_limit_bytes=40 * 2**20
        ),
    )(masked, acts, taps)
    input_grad = ig.reshape(cl, depth, H, W)
    kernel_grad = kg.reshape(3, 3, 3, fl, J * cl).transpose(3, 4, 0, 1, 2)
    return (input_grad, kernel_grad)


def solution(mesh):
    in_specs = (
        P("filt", "space", None, None),
        P("filt", None, None, None, None),
        P("filt", "space", None, None),
        P("filt", "space", None, None),
    )
    out_specs = (P("filt", "space", None, None), P("filt", None, None, None, None))
    return jax.shard_map(
        on_device, mesh=mesh, in_specs=in_specs, out_specs=out_specs, check_vma=False
    )
```

```python
import functools

import jax
import jax.numpy as jnp
from jax import lax
from jax.experimental import pallas as pl
from jax.experimental.pallas import tpu as pltpu
from jax.sharding import PartitionSpec as P

MESH = pl.DeviceIdType.MESH
LANES = 128


def kernel_body(
    dims, m_ref, a_ref, k_ref, ig_ref, kg_ref,
    mbuf, abuf, kpart, kbuf, ktr, gbuf, pbuf, hbuf, rbuf, sbuf, obuf,
    m_recv, sp_send, fl_send, spf_send, flf_send, k_send, k_recv,
    pair_send, pair_recv, rs_send, rs_recv, ag_send, ag_recv, sib_send, sib_recv,
):
    S, J, fl, H, R, owners, scale = dims
    s = lax.axis_index("space")
    j = lax.axis_index("filt")
    core = lax.rem(s, 2)
    chip = s // 2
    chips = S // 2
    sibling = s + 1 - 2 * core
    keep = R * owners
    mine = (chip * owners + chips - 1) // chips
    is_owner = jnp.logical_and(mine < owners, (mine * chips) // owners == chip)
    half = (H // 2) * LANES
    cells = H * LANES
    parts = (pl.ds(LANES, half), pl.ds(LANES + half, cells - half))
    k3 = 3 * J * fl
    cl = a_ref.shape[0]

    def valid(d):
        return s > 0 if d < 0 else s < S - 1

    def far(d):
        return core == (0 if d < 0 else 1)

    def peer(p):
        return lax.rem(j + p, J)

    barrier = pltpu.get_barrier_semaphore()
    for d in (-1, 1):
        @pl.when(valid(d))
        def _():
            pl.semaphore_signal(
                barrier, inc=1, device_id={"space": s + d, "filt": j}, device_id_type=MESH
            )

    @pl.loop(1, chips * J)
    def _(step):
        other = lax.rem(chip * J + j + step, chips * J)
        pl.semaphore_signal(
            barrier, inc=1,
            device_id={"space": 2 * (other // J) + core, "filt": lax.rem(other, J)},
            device_id_type=MESH,
        )

    edge = jnp.zeros((3, J, fl, LANES), jnp.bfloat16)
    mbuf[:, :, :, :LANES] = edge
    mbuf[:, :, :, LANES + cells :] = edge
    mbuf[1, j, :, LANES : LANES + cells] = m_ref[...]

    @pl.when(s == 0)
    def _():
        mbuf[0, :, :, LANES : LANES + cells] = jnp.zeros((J, fl, cells), jnp.bfloat16)

    @pl.when(s == S - 1)
    def _():
        mbuf[2, :, :, LANES : LANES + cells] = jnp.zeros((J, fl, cells), jnp.bfloat16)

    next_to = (s > 0).astype(jnp.int32) + (s < S - 1).astype(jnp.int32)
    pl.semaphore_wait(barrier, chips * J - 1 + next_to)

    def slab_copy(slot, owner, part, to_slot, space, filt, send):
        return pltpu.make_async_remote_copy(
            src_ref=mbuf.at[slot, owner, :, parts[part]],
            dst_ref=mbuf.at[to_slot, owner, :, parts[part]],
            send_sem=send,
            recv_sem=m_recv.at[to_slot, owner, part],
            device_id={"space": space, "filt": filt},
            device_id_type=MESH,
        )

    def arrived(slot, owner, part):
        ref = mbuf.at[slot, owner, :, parts[part]]
        pltpu.make_async_copy(ref, ref, m_recv.at[slot, owner, part]).wait()

    def k_copy(p):
        return pltpu.make_async_remote_copy(
            src_ref=kpart.at[peer(p)], dst_ref=kbuf.at[j],
            send_sem=k_send.at[p - 1], recv_sem=k_recv.at[j],
            device_id={"space": s, "filt": peer(p)}, device_id_type=MESH,
        )

    def space_copy(d, part):
        return slab_copy(1, j, part, 1 - d, s + d, j, sp_send.at[(d + 1) // 2, part])

    def filt_copy(p, part):
        return slab_copy(1, j, part, 1, s, peer(p), fl_send.at[p - 1, part])

    def space_forward(d, p, part):
        return slab_copy(
            1, peer(p), part, 1 - d, s + d, j, spf_send.at[(d + 1) // 2, p - 1, part]
        )

    def filt_forward(d, p):
        return slab_copy(1 + d, j, 0, 1 + d, s, peer(p), flf_send.at[(d + 1) // 2, p - 1])

    for first in (0, 1):
        for p in range(1, J):
            filt_copy(p, 1 - first).start()
        for d in (-1, 1):
            @pl.when(valid(d))
            def _():
                space_copy(d, first).start()

    abuf[:LANES] = jnp.zeros((LANES, LANES), jnp.bfloat16)
    abuf[LANES + cells :] = jnp.zeros((LANES, LANES), jnp.bfloat16)
    gbuf[...] = jnp.zeros_like(gbuf)
    column = lax.broadcasted_iota(jnp.int32, (cl, LANES), 1)

    @pl.loop(0, H)
    def _(row):
        base = pl.multiple_of(row * LANES, LANES)
        x = a_ref[:, pl.ds(base, LANES)].astype(jnp.float32)
        left = jnp.where(column == 0, 0.0, pltpu.roll(x, 1, 1))
        right = jnp.where(column == LANES - 1, 0.0, pltpu.roll(x, LANES - 1, 1))
        rest = jnp.zeros((LANES - 3 * cl, LANES), jnp.float32)
        stacked = jnp.concatenate([left, x, right, rest], axis=0)
        to = pl.ds(pl.multiple_of(row * LANES + LANES, LANES), LANES)
        abuf[to, :] = stacked.T.astype(jnp.bfloat16)

    for q in range(J):
        for dh in range(3):
            for slot in range(3):
                taps = [
                    k_ref[(2 - slot) * 9 + dh * 3 + dw].astype(jnp.float32)[
                        :, q * cl : (q + 1) * cl
                    ]
                    for dw in range(3)
                ]
                taps.append(jnp.zeros((fl, LANES - 3 * cl), jnp.float32))
                kpart[q, dh, slot] = jnp.concatenate(taps, axis=1).astype(jnp.bfloat16)
    for p in range(1, J):
        k_copy(p).start()
    kbuf[j] = kpart[j]

    def weight_terms(pieces, part):
        rows = H // 4

        @pl.loop(2 * part, 2 * part + 2)
        def _(i):
            base = pl.multiple_of(i * rows * LANES, LANES)
            lhs = jnp.concatenate(
                [mbuf[slot, q, :, pl.ds(base + LANES, rows * LANES)] for slot, q in pieces],
                axis=0,
            )
            rhs = jnp.concatenate(
                [abuf[pl.ds(base + dh * LANES, rows * LANES), :] for dh in range(3)], axis=1
            )
            term = jnp.dot(lhs, rhs, preferred_element_type=jnp.float32)
            for dh in range(3):
                for n, (slot, q) in enumerate(pieces):
                    to = slice((dh * 3 + slot) * fl, (dh * 3 + slot + 1) * fl)
                    gbuf[q, to, :] = gbuf[q, to, :] + term[
                        n * fl : (n + 1) * fl, dh * LANES : (dh + 1) * LANES
                    ]

    def pair_copy(p):
        rows_out = pl.ds(pl.multiple_of((1 - core) * keep, 8), keep)
        return pltpu.make_async_remote_copy(
            src_ref=gbuf.at[peer(p), rows_out], dst_ref=pbuf.at[p],
            send_sem=pair_send.at[p], recv_sem=pair_recv.at[p],
            device_id={"space": sibling, "filt": j}, device_id_type=MESH,
        )

    def rs_copy(p, o):
        return pltpu.make_async_remote_copy(
            src_ref=hbuf.at[p, pl.ds(pl.multiple_of(o * R, 8), R)],
            dst_ref=rbuf.at[j, chip],
            send_sem=rs_send.at[p, o], recv_sem=rs_recv.at[j],
            device_id={"space": 2 * ((o * chips) // owners) + core, "filt": peer(p)},
            device_id_type=MESH,
        )

    def rs_each(p, act):
        @pl.loop(0, owners)
        def _(step):
            o = lax.rem(mine + step, owners)
            if p > 0:
                act(rs_copy(p, o))
            else:
                @pl.when((o * chips) // owners != chip)
                def _():
                    act(rs_copy(p, o))

    def ag_copy(p, t):
        return pltpu.make_async_remote_copy(
            src_ref=sbuf.at[p], dst_ref=obuf.at[peer(p), core, mine],
            send_sem=ag_send.at[p, t], recv_sem=ag_recv.at[peer(p)],
            device_id={"space": 2 * t + core, "filt": j}, device_id_type=MESH,
        )

    def ag_each(p, act):
        @pl.loop(1, chips)
        def _(step):
            act(ag_copy(p, lax.rem(chip + step, chips)))

    def sib_copy(p):
        ref = obuf.at[peer(p), core]
        return pltpu.make_async_remote_copy(
            src_ref=ref, dst_ref=ref,
            send_sem=sib_send.at[p], recv_sem=sib_recv.at[peer(p)],
            device_id={"space": sibling, "filt": j}, device_id_type=MESH,
        )

    def pair_start(stage):
        for p in stage:
            pair_copy(p).start()

    def reduce_start(stage):
        for p in stage:
            pair_copy(p).wait_recv()
            own_rows = pl.ds(pl.multiple_of(core * keep, 8), keep)
            hbuf[p] = gbuf[peer(p), own_rows] + pbuf[p]
            rs_each(p, lambda c: c.start())
            if p == 0:
                @pl.when(is_owner)
                def _():
                    pltpu.make_async_copy(
                        hbuf.at[0, pl.ds(pl.multiple_of(mine * R, 8), R)],
                        rbuf.at[j, chip], rs_recv.at[j],
                    ).start()

    def gather_start(stage):
        @pl.when(is_owner)
        def _():
            for p in stage:
                got = rbuf.at[peer(p)]
                pltpu.make_async_copy(got, got, rs_recv.at[peer(p)]).wait()
                total = rbuf[peer(p), 0]
                for t in range(1, chips):
                    total = total + rbuf[peer(p), t]
                sbuf[p] = total * scale
                ag_each(p, lambda c: c.start())
                pltpu.make_async_copy(
                    sbuf.at[p], obuf.at[peer(p), core, mine], ag_recv.at[peer(p)]
                ).start()

    def share_start(stage):
        for p in stage:
            got = obuf.at[peer(p), core]
            pltpu.make_async_copy(got, got, ag_recv.at[peer(p)]).wait()
            sib_copy(p).start()

    early, late = range(0, 1), range(1, J)
    own_all = [(slot, j) for slot in range(3)]
    other_all = [(slot, peer(p)) for p in late for slot in range(3)]

    for p in range(1, J):
        arrived(1, peer(p), 1)
        for d in (-1, 1):
            @pl.when(valid(d))
            def _():
                space_forward(d, p, 1).start()
    for d in (-1, 1):
        @pl.when(valid(d))
        def _():
            arrived(1 + d, j, 0)

            @pl.when(far(d))
            def _():
                for p in range(1, J):
                    filt_forward(d, p).start()
    weight_terms(own_all, 0)
    for p in range(1, J):
        arrived(1, peer(p), 0)
        for d in (-1, 1):
            @pl.when(jnp.logical_and(valid(d), jnp.logical_not(far(d))))
            def _():
                space_forward(d, p, 0).start()
    for d in (-1, 1):
        @pl.when(valid(d))
        def _():
            arrived(1 + d, j, 1)
    weight_terms(own_all, 1)
    pair_start(early)

    for p in range(1, J):
        got = kbuf.at[peer(p)]
        pltpu.make_async_copy(got, got, k_recv.at[peer(p)]).wait()
    stacked = jnp.concatenate(
        [kbuf[q, dh, slot] for dh in range(3) for slot in range(3) for q in range(J)], axis=0
    )
    ktr[...] = stacked.astype(jnp.float32).T.astype(jnp.bfloat16)
    reduce_start(early)

    for part in (1, 0):
        for d in (-1, 1):
            @pl.when(valid(d))
            def _():
                for p in range(1, J):
                    arrived(1 + d, peer(p), part)
        if J > 1:
            weight_terms(other_all, part)
        if part == 1:
            gather_start(early)
    pair_start(late)

    rows = H // 8
    wide = rows * LANES
    cols = lax.rem(lax.broadcasted_iota(jnp.int32, (cl, wide), 1), LANES)

    def input_part(first_step, last_step):
        @pl.loop(first_step, last_step)
        def _(i):
            for sub in range(2):
                at = (2 * i + sub) * rows
                slabs = [
                    mbuf[
                        :, :, :, pl.ds(pl.multiple_of((at + 2 - dh) * LANES, LANES), wide)
                    ].reshape(k3, wide)
                    for dh in range(3)
                ]
                total = jnp.dot(
                    ktr[: 3 * cl], jnp.concatenate(slabs, axis=0),
                    preferred_element_type=jnp.float32,
                )
                first = pltpu.roll(total[:cl], wide - 1, 1)
                last = pltpu.roll(total[2 * cl :], 1, 1)
                result = total[cl : 2 * cl] + jnp.where(cols == LANES - 1, 0.0, first)
                result = result + jnp.where(cols == 0, 0.0, last)
                to = pl.ds(pl.multiple_of(at * LANES, LANES), wide)
                ig_ref[:, to] = result.astype(jnp.bfloat16)

    input_part(0, 1)
    reduce_start(late)
    input_part(1, 2)
    share_start(early)
    input_part(2, 3)
    gather_start(late)
    input_part(3, 4)
    share_start(late)
    for p in range(J):
        sib_copy(p).wait_recv()
    blocks = [obuf[q].reshape(2 * keep, LANES) for q in range(J)]
    for dh in range(3):
        for slot in range(3):
            at = (dh * 3 + slot) * fl
            for dw in range(3):
                kg_ref[(2 - slot) * 9 + dh * 3 + dw] = jnp.concatenate(
                    [b[at : at + fl, dw * cl : (dw + 1) * cl] for b in blocks], axis=1
                )

    for first in (0, 1):
        for p in range(1, J):
            filt_copy(p, 1 - first).wait_send()
        for d in (-1, 1):
            @pl.when(valid(d))
            def _():
                space_copy(d, first).wait_send()
    for p in range(1, J):
        k_copy(p).wait_send()
        for d in (-1, 1):
            @pl.when(valid(d))
            def _():
                space_forward(d, p, 1).wait_send()

                @pl.when(far(d))
                def _():
                    filt_forward(d, p).wait_send()

                @pl.when(jnp.logical_not(far(d)))
                def _():
                    space_forward(d, p, 0).wait_send()
    for p in range(J):
        pair_copy(p).wait_send()
        rs_each(p, lambda c: c.wait_send())

        @pl.when(is_owner)
        def _():
            ag_each(p, lambda c: c.wait_send())

        sib_copy(p).wait_send()


def on_device(activations, kernel, preact, upstream):
    S, J = lax.axis_size("space"), lax.axis_size("filt")
    fl, depth, H, W = preact.shape
    cl = activations.shape[0]
    cells = H * W
    volume = S * depth * cells
    scale = 1.0 / float(volume) ** 0.5
    masked = jnp.where(preact > 0, upstream, jnp.zeros_like(upstream)).reshape(fl, cells)
    acts = activations.reshape(cl, cells)
    taps = kernel.transpose(2, 3, 4, 0, 1).reshape(27, fl, J * cl)
    chips = S // 2
    tiles = -(-9 * fl // 16)
    R = 8 * -(-tiles // chips)
    owners = -(-8 * tiles // R)
    keep = R * owners
    dims = (S, J, fl, H, R, owners, scale)
    padded = cells + 2 * W
    dma = pltpu.SemaphoreType.DMA
    vmem = pl.BlockSpec(memory_space=pltpu.VMEM)
    peers = max(J - 1, 1)
    ig, kg = pl.pallas_call(
        functools.partial(kernel_body, dims),
        out_shape=(
            jax.ShapeDtypeStruct((cl, cells), jnp.bfloat16),
            jax.ShapeDtypeStruct((27, fl, J * cl), jnp.float32),
        ),
        in_specs=[vmem] * 3,
        out_specs=(vmem, vmem),
        scratch_shapes=[
            pltpu.VMEM((3, J, fl, padded), jnp.bfloat16),
            pltpu.VMEM((padded, LANES), jnp.bfloat16),
            pltpu.VMEM((J, 3, 3, fl, LANES), jnp.bfloat16),
            pltpu.VMEM((J, 3, 3, fl, LANES), jnp.bfloat16),
            pltpu.VMEM((LANES, 9 * J * fl), jnp.bfloat16),
            pltpu.VMEM((J, 2 * keep, LANES), jnp.float32),
            pltpu.VMEM((J, keep, LANES), jnp.float32),
            pltpu.VMEM((J, keep, LANES), jnp.float32),
            pltpu.VMEM((J, chips, R, LANES), jnp.float32),
            pltpu.VMEM((J, R, LANES), jnp.float32),
            pltpu.VMEM((J, 2, owners, R, LANES), jnp.float32),
            dma((3, J, 2)), dma((2, 2)), dma((peers, 2)), dma((2, peers, 2)),
            dma((2, peers)), dma((peers,)), dma((J,)),
            dma((J,)), dma((J,)), dma((J, owners)), dma((J,)), dma((J, chips)), dma((J,)),
            dma((J,)), dma((J,)),
        ],
        compiler_params=pltpu.CompilerParams(
            collective_id=0, has_side_effects=True, vmem_limit_bytes=40 * 2**20
        ),
    )(masked, acts, taps)
    input_grad = ig.reshape(cl, depth, H, W)
    kernel_grad = kg.reshape(3, 3, 3, fl, J * cl).transpose(3, 4, 0, 1, 2)
    return (input_grad, kernel_grad)


def solution(mesh):
    in_specs = (
        P("filt", "space", None, None),
        P("filt", None, None, None, None),
        P("filt", "space", None, None),
        P("filt", "space", None, None),
    )
    out_specs = (P("filt", "space", None, None), P("filt", None, None, None, None))
    return jax.shard_map(
        on_device, mesh=mesh, in_specs=in_specs, out_specs=out_specs, check_vma=False
    )
```

```python
import functools

import jax
import jax.numpy as jnp
from jax import lax
from jax.experimental import pallas as pl
from jax.experimental.pallas import tpu as pltpu
from jax.sharding import PartitionSpec as P

MESH = pl.DeviceIdType.MESH
LANES = 128


def kernel_body(
    dims, m_ref, a_ref, k_ref, ig_ref, kg_ref,
    mbuf, abuf, kpart, kbuf, ktr, gbuf, pbuf, hbuf, rbuf, sbuf, obuf,
    m_recv, sp_send, fl_send, spf_send, flf_send, k_send, k_recv,
    pair_send, pair_recv, rs_send, rs_recv, ag_send, ag_recv, sib_send, sib_recv,
):
    S, J, fl, H, R, owners, scale = dims
    s = lax.axis_index("space")
    j = lax.axis_index("filt")
    core = lax.rem(s, 2)
    chip = s // 2
    chips = S // 2
    sibling = s + 1 - 2 * core
    keep = R * owners
    mine = (chip * owners + chips - 1) // chips
    is_owner = jnp.logical_and(mine < owners, (mine * chips) // owners == chip)
    half = (H // 2) * LANES
    cells = H * LANES
    parts = (pl.ds(LANES, half), pl.ds(LANES + half, cells - half))
    k3 = 3 * J * fl
    cl = a_ref.shape[0]

    def valid(d):
        return s > 0 if d < 0 else s < S - 1

    def far(d):
        return core == (0 if d < 0 else 1)

    def peer(p):
        return lax.rem(j + p, J)

    barrier = pltpu.get_barrier_semaphore()
    for d in (-1, 1):
        @pl.when(valid(d))
        def _():
            pl.semaphore_signal(
                barrier, inc=1, device_id={"space": s + d, "filt": j}, device_id_type=MESH
            )

    @pl.loop(1, chips * J)
    def _(step):
        other = lax.rem(chip * J + j + step, chips * J)
        pl.semaphore_signal(
            barrier, inc=1,
            device_id={"space": 2 * (other // J) + core, "filt": lax.rem(other, J)},
            device_id_type=MESH,
        )

    next_to = (s > 0).astype(jnp.int32) + (s < S - 1).astype(jnp.int32)
    pl.semaphore_wait(barrier, chips * J - 1 + next_to)

    def slab_copy(slot, owner, part, to_slot, space, filt, send):
        return pltpu.make_async_remote_copy(
            src_ref=mbuf.at[slot, owner, :, parts[part]],
            dst_ref=mbuf.at[to_slot, owner, :, parts[part]],
            send_sem=send,
            recv_sem=m_recv.at[to_slot, owner, part],
            device_id={"space": space, "filt": filt},
            device_id_type=MESH,
        )

    def arrived(slot, owner, part):
        ref = mbuf.at[slot, owner, :, parts[part]]
        pltpu.make_async_copy(ref, ref, m_recv.at[slot, owner, part]).wait()

    def k_copy(p):
        return pltpu.make_async_remote_copy(
            src_ref=kpart.at[peer(p)], dst_ref=kbuf.at[j],
            send_sem=k_send.at[p - 1], recv_sem=k_recv.at[j],
            device_id={"space": s, "filt": peer(p)}, device_id_type=MESH,
        )

    def own_copy(part, to_slot, space, filt, send):
        return pltpu.make_async_remote_copy(
            src_ref=m_ref.at[:, (pl.ds(0, half), pl.ds(half, cells - half))[part]],
            dst_ref=mbuf.at[to_slot, j, :, parts[part]],
            send_sem=send,
            recv_sem=m_recv.at[to_slot, j, part],
            device_id={"space": space, "filt": filt},
            device_id_type=MESH,
        )

    def space_copy(d, part):
        return own_copy(part, 1 - d, s + d, j, sp_send.at[(d + 1) // 2, part])

    def filt_copy(p, part):
        return own_copy(part, 1, s, peer(p), fl_send.at[p - 1, part])

    def space_forward(d, p, part):
        return slab_copy(
            1, peer(p), part, 1 - d, s + d, j, spf_send.at[(d + 1) // 2, p - 1, part]
        )

    def filt_forward(d, p):
        return slab_copy(1 + d, j, 0, 1 + d, s, peer(p), flf_send.at[(d + 1) // 2, p - 1])

    for first in (0, 1):
        for p in range(1, J):
            filt_copy(p, 1 - first).start()
        for d in (-1, 1):
            @pl.when(valid(d))
            def _():
                space_copy(d, first).start()

    edge = jnp.zeros((3, J, fl, LANES), jnp.bfloat16)
    mbuf[:, :, :, :LANES] = edge
    mbuf[:, :, :, LANES + cells :] = edge
    mbuf[1, j, :, LANES : LANES + cells] = m_ref[...]

    @pl.when(s == 0)
    def _():
        mbuf[0, :, :, LANES : LANES + cells] = jnp.zeros((J, fl, cells), jnp.bfloat16)

    @pl.when(s == S - 1)
    def _():
        mbuf[2, :, :, LANES : LANES + cells] = jnp.zeros((J, fl, cells), jnp.bfloat16)

    abuf[:LANES] = jnp.zeros((LANES, LANES), jnp.bfloat16)
    abuf[LANES + cells :] = jnp.zeros((LANES, LANES), jnp.bfloat16)
    gbuf[...] = jnp.zeros_like(gbuf)
    column = lax.broadcasted_iota(jnp.int32, (cl, LANES), 1)

    group = 8 if H % 8 == 0 else 1

    @pl.loop(0, H // group)
    def _(i):
        base = pl.multiple_of(i * group * LANES, LANES)
        wide_x = a_ref[:, pl.ds(base, group * LANES)].astype(jnp.float32)
        rest = jnp.zeros((LANES - 3 * cl, LANES), jnp.float32)
        for row in range(group):
            x = wide_x[:, row * LANES : (row + 1) * LANES]
            left = jnp.where(column == 0, 0.0, pltpu.roll(x, 1, 1))
            right = jnp.where(column == LANES - 1, 0.0, pltpu.roll(x, LANES - 1, 1))
            stacked = jnp.concatenate([left, x, right, rest], axis=0)
            to = pl.ds(pl.multiple_of(base + (row + 1) * LANES, LANES), LANES)
            abuf[to, :] = stacked.T.astype(jnp.bfloat16)

    for q in range(J):
        for dh in range(3):
            for slot in range(3):
                taps = [
                    k_ref[(2 - slot) * 9 + dh * 3 + dw].astype(jnp.float32)[
                        :, q * cl : (q + 1) * cl
                    ]
                    for dw in range(3)
                ]
                taps.append(jnp.zeros((fl, LANES - 3 * cl), jnp.float32))
                kpart[q, dh, slot] = jnp.concatenate(taps, axis=1).astype(jnp.bfloat16)
    for p in range(1, J):
        k_copy(p).start()
    kbuf[j] = kpart[j]

    def weight_terms(pieces, part):
        rows = H // 4

        @pl.loop(2 * part, 2 * part + 2)
        def _(i):
            base = pl.multiple_of(i * rows * LANES, LANES)
            lhs = jnp.concatenate(
                [mbuf[slot, q, :, pl.ds(base + LANES, rows * LANES)] for slot, q in pieces],
                axis=0,
            )
            rhs = jnp.concatenate(
                [abuf[pl.ds(base + dh * LANES, rows * LANES), :] for dh in range(3)], axis=1
            )
            term = jnp.dot(lhs, rhs, preferred_element_type=jnp.float32)
            for dh in range(3):
                for n, (slot, q) in enumerate(pieces):
                    to = slice((dh * 3 + slot) * fl, (dh * 3 + slot + 1) * fl)
                    gbuf[q, to, :] = gbuf[q, to, :] + term[
                        n * fl : (n + 1) * fl, dh * LANES : (dh + 1) * LANES
                    ]

    def pair_copy(p):
        rows_out = pl.ds(pl.multiple_of((1 - core) * keep, 8), keep)
        return pltpu.make_async_remote_copy(
            src_ref=gbuf.at[peer(p), rows_out], dst_ref=pbuf.at[p],
            send_sem=pair_send.at[p], recv_sem=pair_recv.at[p],
            device_id={"space": sibling, "filt": j}, device_id_type=MESH,
        )

    def rs_copy(p, o):
        return pltpu.make_async_remote_copy(
            src_ref=hbuf.at[p, pl.ds(pl.multiple_of(o * R, 8), R)],
            dst_ref=rbuf.at[j, chip],
            send_sem=rs_send.at[p, o], recv_sem=rs_recv.at[j],
            device_id={"space": 2 * ((o * chips) // owners) + core, "filt": peer(p)},
            device_id_type=MESH,
        )

    def rs_each(p, act):
        @pl.loop(0, owners)
        def _(step):
            o = lax.rem(mine + step, owners)
            if p > 0:
                act(rs_copy(p, o))
            else:
                @pl.when((o * chips) // owners != chip)
                def _():
                    act(rs_copy(p, o))

    def ag_copy(p, t):
        return pltpu.make_async_remote_copy(
            src_ref=sbuf.at[p], dst_ref=obuf.at[peer(p), core, mine],
            send_sem=ag_send.at[p, t], recv_sem=ag_recv.at[peer(p)],
            device_id={"space": 2 * t + core, "filt": j}, device_id_type=MESH,
        )

    def ag_each(p, act):
        @pl.loop(1, chips)
        def _(step):
            act(ag_copy(p, lax.rem(chip + step, chips)))

    def sib_copy(p):
        ref = obuf.at[peer(p), core]
        return pltpu.make_async_remote_copy(
            src_ref=ref, dst_ref=ref,
            send_sem=sib_send.at[p], recv_sem=sib_recv.at[peer(p)],
            device_id={"space": sibling, "filt": j}, device_id_type=MESH,
        )

    def pair_start(stage):
        for p in stage:
            pair_copy(p).start()

    def reduce_start(stage):
        for p in stage:
            pair_copy(p).wait_recv()
            own_rows = pl.ds(pl.multiple_of(core * keep, 8), keep)
            hbuf[p] = gbuf[peer(p), own_rows] + pbuf[p]
            rs_each(p, lambda c: c.start())
            if p == 0:
                @pl.when(is_owner)
                def _():
                    pltpu.make_async_copy(
                        hbuf.at[0, pl.ds(pl.multiple_of(mine * R, 8), R)],
                        rbuf.at[j, chip], rs_recv.at[j],
                    ).start()

    def gather_start(stage):
        @pl.when(is_owner)
        def _():
            for p in stage:
                got = rbuf.at[peer(p)]
                pltpu.make_async_copy(got, got, rs_recv.at[peer(p)]).wait()
                total = rbuf[peer(p), 0]
                for t in range(1, chips):
                    total = total + rbuf[peer(p), t]
                sbuf[p] = total * scale
                ag_each(p, lambda c: c.start())
                pltpu.make_async_copy(
                    sbuf.at[p], obuf.at[peer(p), core, mine], ag_recv.at[peer(p)]
                ).start()

    def share_start(stage):
        for p in stage:
            got = obuf.at[peer(p), core]
            pltpu.make_async_copy(got, got, ag_recv.at[peer(p)]).wait()
            sib_copy(p).start()

    early, late = range(0, 1), range(1, J)
    own_all = [(slot, j) for slot in range(3)]
    other_all = [(slot, peer(p)) for p in late for slot in range(3)]

    for p in range(1, J):
        arrived(1, peer(p), 1)
        for d in (-1, 1):
            @pl.when(valid(d))
            def _():
                space_forward(d, p, 1).start()
    for d in (-1, 1):
        @pl.when(valid(d))
        def _():
            arrived(1 + d, j, 0)

            @pl.when(far(d))
            def _():
                for p in range(1, J):
                    filt_forward(d, p).start()
    weight_terms(own_all, 0)
    for p in range(1, J):
        arrived(1, peer(p), 0)
        for d in (-1, 1):
            @pl.when(jnp.logical_and(valid(d), jnp.logical_not(far(d))))
            def _():
                space_forward(d, p, 0).start()
    for d in (-1, 1):
        @pl.when(valid(d))
        def _():
            arrived(1 + d, j, 1)
    weight_terms(own_all, 1)
    pair_start(early)

    for p in range(1, J):
        got = kbuf.at[peer(p)]
        pltpu.make_async_copy(got, got, k_recv.at[peer(p)]).wait()
    stacked = jnp.concatenate(
        [kbuf[q, dh, slot] for dh in range(3) for slot in range(3) for q in range(J)], axis=0
    )
    ktr[...] = stacked.astype(jnp.float32).T.astype(jnp.bfloat16)
    reduce_start(early)

    for part in (1, 0):
        for d in (-1, 1):
            @pl.when(valid(d))
            def _():
                for p in range(1, J):
                    arrived(1 + d, peer(p), part)
        if J > 1:
            weight_terms(other_all, part)
        if part == 1:
            gather_start(early)
    pair_start(late)

    rows = H // 8
    wide = rows * LANES
    cols = lax.rem(lax.broadcasted_iota(jnp.int32, (cl, wide), 1), LANES)

    def input_part(first_step, last_step):
        @pl.loop(first_step, last_step)
        def _(i):
            for sub in range(2):
                at = (2 * i + sub) * rows
                slabs = [
                    mbuf[
                        :, :, :, pl.ds(pl.multiple_of((at + 2 - dh) * LANES, LANES), wide)
                    ].reshape(k3, wide)
                    for dh in range(3)
                ]
                total = jnp.dot(
                    ktr[: 3 * cl], jnp.concatenate(slabs, axis=0),
                    preferred_element_type=jnp.float32,
                )
                first = pltpu.roll(total[:cl], wide - 1, 1)
                last = pltpu.roll(total[2 * cl :], 1, 1)
                result = total[cl : 2 * cl] + jnp.where(cols == LANES - 1, 0.0, first)
                result = result + jnp.where(cols == 0, 0.0, last)
                to = pl.ds(pl.multiple_of(at * LANES, LANES), wide)
                ig_ref[:, to] = result.astype(jnp.bfloat16)

    input_part(0, 1)
    reduce_start(late)
    input_part(1, 2)
    share_start(early)
    input_part(2, 3)
    gather_start(late)
    input_part(3, 4)
    share_start(late)
    for p in range(J):
        sib_copy(p).wait_recv()
    blocks = [obuf[q].reshape(2 * keep, LANES) for q in range(J)]
    for dh in range(3):
        for slot in range(3):
            at = (dh * 3 + slot) * fl
            for dw in range(3):
                kg_ref[(2 - slot) * 9 + dh * 3 + dw] = jnp.concatenate(
                    [b[at : at + fl, dw * cl : (dw + 1) * cl] for b in blocks], axis=1
                )

    for first in (0, 1):
        for p in range(1, J):
            filt_copy(p, 1 - first).wait_send()
        for d in (-1, 1):
            @pl.when(valid(d))
            def _():
                space_copy(d, first).wait_send()
    for p in range(1, J):
        k_copy(p).wait_send()
        for d in (-1, 1):
            @pl.when(valid(d))
            def _():
                space_forward(d, p, 1).wait_send()

                @pl.when(far(d))
                def _():
                    filt_forward(d, p).wait_send()

                @pl.when(jnp.logical_not(far(d)))
                def _():
                    space_forward(d, p, 0).wait_send()
    for p in range(J):
        pair_copy(p).wait_send()
        rs_each(p, lambda c: c.wait_send())

        @pl.when(is_owner)
        def _():
            ag_each(p, lambda c: c.wait_send())

        sib_copy(p).wait_send()


def on_device(activations, kernel, preact, upstream):
    S, J = lax.axis_size("space"), lax.axis_size("filt")
    fl, depth, H, W = preact.shape
    cl = activations.shape[0]
    cells = H * W
    volume = S * depth * cells
    scale = 1.0 / float(volume) ** 0.5
    masked = jnp.where(preact > 0, upstream, jnp.zeros_like(upstream)).reshape(fl, cells)
    acts = activations.reshape(cl, cells)
    taps = kernel.transpose(2, 3, 4, 0, 1).reshape(27, fl, J * cl)
    chips = S // 2
    tiles = -(-9 * fl // 16)
    R = 8 * -(-tiles // chips)
    owners = -(-8 * tiles // R)
    keep = R * owners
    dims = (S, J, fl, H, R, owners, scale)
    padded = cells + 2 * W
    dma = pltpu.SemaphoreType.DMA
    vmem = pl.BlockSpec(memory_space=pltpu.VMEM)
    peers = max(J - 1, 1)
    ig, kg = pl.pallas_call(
        functools.partial(kernel_body, dims),
        out_shape=(
            jax.ShapeDtypeStruct((cl, cells), jnp.bfloat16),
            jax.ShapeDtypeStruct((27, fl, J * cl), jnp.float32),
        ),
        in_specs=[vmem] * 3,
        out_specs=(vmem, vmem),
        scratch_shapes=[
            pltpu.VMEM((3, J, fl, padded), jnp.bfloat16),
            pltpu.VMEM((padded, LANES), jnp.bfloat16),
            pltpu.VMEM((J, 3, 3, fl, LANES), jnp.bfloat16),
            pltpu.VMEM((J, 3, 3, fl, LANES), jnp.bfloat16),
            pltpu.VMEM((LANES, 9 * J * fl), jnp.bfloat16),
            pltpu.VMEM((J, 2 * keep, LANES), jnp.float32),
            pltpu.VMEM((J, keep, LANES), jnp.float32),
            pltpu.VMEM((J, keep, LANES), jnp.float32),
            pltpu.VMEM((J, chips, R, LANES), jnp.float32),
            pltpu.VMEM((J, R, LANES), jnp.float32),
            pltpu.VMEM((J, 2, owners, R, LANES), jnp.float32),
            dma((3, J, 2)), dma((2, 2)), dma((peers, 2)), dma((2, peers, 2)),
            dma((2, peers)), dma((peers,)), dma((J,)),
            dma((J,)), dma((J,)), dma((J, owners)), dma((J,)), dma((J, chips)), dma((J,)),
            dma((J,)), dma((J,)),
        ],
        compiler_params=pltpu.CompilerParams(
            collective_id=0, has_side_effects=True, vmem_limit_bytes=40 * 2**20
        ),
    )(masked, acts, taps)
    input_grad = ig.reshape(cl, depth, H, W)
    kernel_grad = kg.reshape(3, 3, 3, fl, J * cl).transpose(3, 4, 0, 1, 2)
    return (input_grad, kernel_grad)


def solution(mesh):
    in_specs = (
        P("filt", "space", None, None),
        P("filt", None, None, None, None),
        P("filt", "space", None, None),
        P("filt", "space", None, None),
    )
    out_specs = (P("filt", "space", None, None), P("filt", None, None, None, None))
    return jax.shard_map(
        on_device, mesh=mesh, in_specs=in_specs, out_specs=out_specs, check_vma=False
    )
```

```python
import functools

import jax
import jax.numpy as jnp
from jax import lax
from jax.experimental import pallas as pl
from jax.experimental.pallas import tpu as pltpu
from jax.sharding import PartitionSpec as P

MESH = pl.DeviceIdType.MESH
LANES = 128


def kernel_body(
    dims, m_ref, a_ref, k_ref, ig_ref, kg_ref,
    mbuf, abuf, kpart, kbuf, kown, kother, ybuf, gbuf, pbuf, hbuf, rbuf, sbuf, obuf,
    m_recv, sp_send, fl_send, spf_send, flf_send, k_send, k_recv,
    pair_send, pair_recv, rs_send, rs_recv, ag_send, ag_recv, sib_send, sib_recv,
):
    S, J, fl, H, R, owners, scale = dims
    s = lax.axis_index("space")
    j = lax.axis_index("filt")
    core = lax.rem(s, 2)
    chip = s // 2
    chips = S // 2
    sibling = s + 1 - 2 * core
    keep = R * owners
    mine = (chip * owners + chips - 1) // chips
    is_owner = jnp.logical_and(mine < owners, (mine * chips) // owners == chip)
    half = (H // 2) * LANES
    cells = H * LANES
    parts = (pl.ds(LANES, half), pl.ds(LANES + half, cells - half))
    cl = a_ref.shape[0]

    def valid(d):
        return s > 0 if d < 0 else s < S - 1

    def far(d):
        return core == (0 if d < 0 else 1)

    def peer(p):
        return lax.rem(j + p, J)

    barrier = pltpu.get_barrier_semaphore()
    for d in (-1, 1):
        @pl.when(valid(d))
        def _():
            pl.semaphore_signal(
                barrier, inc=1, device_id={"space": s + d, "filt": j}, device_id_type=MESH
            )

    @pl.loop(1, chips * J)
    def _(step):
        other = lax.rem(chip * J + j + step, chips * J)
        pl.semaphore_signal(
            barrier, inc=1,
            device_id={"space": 2 * (other // J) + core, "filt": lax.rem(other, J)},
            device_id_type=MESH,
        )

    edge = jnp.zeros((3, J, fl, LANES), jnp.bfloat16)
    mbuf[:, :, :, :LANES] = edge
    mbuf[:, :, :, LANES + cells :] = edge
    mbuf[1, j, :, LANES : LANES + cells] = m_ref[...]

    @pl.when(s == 0)
    def _():
        mbuf[0, :, :, LANES : LANES + cells] = jnp.zeros((J, fl, cells), jnp.bfloat16)

    @pl.when(s == S - 1)
    def _():
        mbuf[2, :, :, LANES : LANES + cells] = jnp.zeros((J, fl, cells), jnp.bfloat16)

    next_to = (s > 0).astype(jnp.int32) + (s < S - 1).astype(jnp.int32)
    pl.semaphore_wait(barrier, chips * J - 1 + next_to)

    def slab_copy(slot, owner, part, to_slot, space, filt, send):
        return pltpu.make_async_remote_copy(
            src_ref=mbuf.at[slot, owner, :, parts[part]],
            dst_ref=mbuf.at[to_slot, owner, :, parts[part]],
            send_sem=send,
            recv_sem=m_recv.at[to_slot, owner, part],
            device_id={"space": space, "filt": filt},
            device_id_type=MESH,
        )

    def arrived(slot, owner, part):
        ref = mbuf.at[slot, owner, :, parts[part]]
        pltpu.make_async_copy(ref, ref, m_recv.at[slot, owner, part]).wait()

    def k_copy(p):
        return pltpu.make_async_remote_copy(
            src_ref=kpart.at[peer(p)], dst_ref=kbuf.at[j],
            send_sem=k_send.at[p - 1], recv_sem=k_recv.at[j],
            device_id={"space": s, "filt": peer(p)}, device_id_type=MESH,
        )

    def space_copy(d, part):
        return slab_copy(1, j, part, 1 - d, s + d, j, sp_send.at[(d + 1) // 2, part])

    def filt_copy(p, part):
        return slab_copy(1, j, part, 1, s, peer(p), fl_send.at[p - 1, part])

    def space_forward(d, p, part):
        return slab_copy(
            1, peer(p), part, 1 - d, s + d, j, spf_send.at[(d + 1) // 2, p - 1, part]
        )

    def filt_forward(d, p):
        return slab_copy(1 + d, j, 0, 1 + d, s, peer(p), flf_send.at[(d + 1) // 2, p - 1])

    for first in (0, 1):
        for p in range(1, J):
            filt_copy(p, 1 - first).start()
        for d in (-1, 1):
            @pl.when(valid(d))
            def _():
                space_copy(d, first).start()

    abuf[:LANES] = jnp.zeros((LANES, LANES), jnp.bfloat16)
    abuf[LANES + cells :] = jnp.zeros((LANES, LANES), jnp.bfloat16)
    gbuf[...] = jnp.zeros_like(gbuf)
    column = lax.broadcasted_iota(jnp.int32, (cl, LANES), 1)

    @pl.loop(0, H)
    def _(row):
        base = pl.multiple_of(row * LANES, LANES)
        x = a_ref[:, pl.ds(base, LANES)].astype(jnp.float32)
        left = jnp.where(column == 0, 0.0, pltpu.roll(x, 1, 1))
        right = jnp.where(column == LANES - 1, 0.0, pltpu.roll(x, LANES - 1, 1))
        rest = jnp.zeros((LANES - 3 * cl, LANES), jnp.float32)
        stacked = jnp.concatenate([left, x, right, rest], axis=0)
        to = pl.ds(pl.multiple_of(row * LANES + LANES, LANES), LANES)
        abuf[to, :] = stacked.T.astype(jnp.bfloat16)

    for q in range(J):
        for dh in range(3):
            for slot in range(3):
                taps = [
                    k_ref[(2 - slot) * 9 + dh * 3 + dw].astype(jnp.float32)[
                        :, q * cl : (q + 1) * cl
                    ]
                    for dw in range(3)
                ]
                taps.append(jnp.zeros((fl, LANES - 3 * cl), jnp.float32))
                kpart[q, dh, slot] = jnp.concatenate(taps, axis=1).astype(jnp.bfloat16)
    for p in range(1, J):
        k_copy(p).start()

    def weight_terms(pieces, part):
        rows = H // 4

        @pl.loop(2 * part, 2 * part + 2)
        def _(i):
            base = pl.multiple_of(i * rows * LANES, LANES)
            lhs = jnp.concatenate(
                [mbuf[slot, q, :, pl.ds(base + LANES, rows * LANES)] for slot, q in pieces],
                axis=0,
            )
            rhs = jnp.concatenate(
                [abuf[pl.ds(base + dh * LANES, rows * LANES), :] for dh in range(3)], axis=1
            )
            term = jnp.dot(lhs, rhs, preferred_element_type=jnp.float32)
            for dh in range(3):
                for n, (slot, q) in enumerate(pieces):
                    to = slice((dh * 3 + slot) * fl, (dh * 3 + slot + 1) * fl)
                    gbuf[q, to, :] = gbuf[q, to, :] + term[
                        n * fl : (n + 1) * fl, dh * LANES : (dh + 1) * LANES
                    ]

    def pair_copy(p):
        rows_out = pl.ds(pl.multiple_of((1 - core) * keep, 8), keep)
        return pltpu.make_async_remote_copy(
            src_ref=gbuf.at[peer(p), rows_out], dst_ref=pbuf.at[p],
            send_sem=pair_send.at[p], recv_sem=pair_recv.at[p],
            device_id={"space": sibling, "filt": j}, device_id_type=MESH,
        )

    def rs_copy(p, o):
        return pltpu.make_async_remote_copy(
            src_ref=hbuf.at[p, pl.ds(pl.multiple_of(o * R, 8), R)],
            dst_ref=rbuf.at[j, chip],
            send_sem=rs_send.at[p, o], recv_sem=rs_recv.at[j],
            device_id={"space": 2 * ((o * chips) // owners) + core, "filt": peer(p)},
            device_id_type=MESH,
        )

    def rs_each(p, act):
        @pl.loop(0, owners)
        def _(step):
            o = lax.rem(mine + step, owners)
            if p > 0:
                act(rs_copy(p, o))
            else:
                @pl.when((o * chips) // owners != chip)
                def _():
                    act(rs_copy(p, o))

    def ag_copy(p, t):
        return pltpu.make_async_remote_copy(
            src_ref=sbuf.at[p], dst_ref=obuf.at[peer(p), core, mine],
            send_sem=ag_send.at[p, t], recv_sem=ag_recv.at[peer(p)],
            device_id={"space": 2 * t + core, "filt": j}, device_id_type=MESH,
        )

    def ag_each(p, act):
        @pl.loop(1, chips)
        def _(step):
            act(ag_copy(p, lax.rem(chip + step, chips)))

    def sib_copy(p):
        ref = obuf.at[peer(p), core]
        return pltpu.make_async_remote_copy(
            src_ref=ref, dst_ref=ref,
            send_sem=sib_send.at[p], recv_sem=sib_recv.at[peer(p)],
            device_id={"space": sibling, "filt": j}, device_id_type=MESH,
        )

    def pair_start(stage):
        for p in stage:
            pair_copy(p).start()

    def reduce_start(stage):
        for p in stage:
            pair_copy(p).wait_recv()
            own_rows = pl.ds(pl.multiple_of(core * keep, 8), keep)
            hbuf[p] = gbuf[peer(p), own_rows] + pbuf[p]
            rs_each(p, lambda c: c.start())
            if p == 0:
                @pl.when(is_owner)
                def _():
                    pltpu.make_async_copy(
                        hbuf.at[0, pl.ds(pl.multiple_of(mine * R, 8), R)],
                        rbuf.at[j, chip], rs_recv.at[j],
                    ).start()

    def gather_start(stage):
        @pl.when(is_owner)
        def _():
            for p in stage:
                got = rbuf.at[peer(p)]
                pltpu.make_async_copy(got, got, rs_recv.at[peer(p)]).wait()
                total = rbuf[peer(p), 0]
                for t in range(1, chips):
                    total = total + rbuf[peer(p), t]
                sbuf[p] = total * scale
                ag_each(p, lambda c: c.start())
                pltpu.make_async_copy(
                    sbuf.at[p], obuf.at[peer(p), core, mine], ag_recv.at[peer(p)]
                ).start()

    def share_start(stage):
        for p in stage:
            got = obuf.at[peer(p), core]
            pltpu.make_async_copy(got, got, ag_recv.at[peer(p)]).wait()
            sib_copy(p).start()

    early, late = range(0, 1), range(1, J)
    own_all = [(slot, j) for slot in range(3)]
    other_all = [(slot, peer(p)) for p in late for slot in range(3)]

    for p in range(1, J):
        arrived(1, peer(p), 1)
        for d in (-1, 1):
            @pl.when(valid(d))
            def _():
                space_forward(d, p, 1).start()
    for d in (-1, 1):
        @pl.when(valid(d))
        def _():
            arrived(1 + d, j, 0)

            @pl.when(far(d))
            def _():
                for p in range(1, J):
                    filt_forward(d, p).start()
    weight_terms(own_all, 0)
    for p in range(1, J):
        arrived(1, peer(p), 0)
        for d in (-1, 1):
            @pl.when(jnp.logical_and(valid(d), jnp.logical_not(far(d))))
            def _():
                space_forward(d, p, 0).start()
    for d in (-1, 1):
        @pl.when(valid(d))
        def _():
            arrived(1 + d, j, 1)
    weight_terms(own_all, 1)
    pair_start(early)

    def taps_of(blocks):
        return jnp.concatenate(blocks, axis=0).astype(jnp.float32).T.astype(jnp.bfloat16)

    kown[...] = taps_of([kpart[j, dh, slot] for dh in range(3) for slot in range(3)])
    reduce_start(early)

    rows = H // 8
    wide = rows * LANES
    cols = lax.rem(lax.broadcasted_iota(jnp.int32, (cl, wide), 1), LANES)

    def slabs_at(at, pieces):
        return jnp.concatenate(
            [
                mbuf[slot, q, :, pl.ds(pl.multiple_of((at + 2 - dh) * LANES, LANES), wide)]
                for dh in range(3)
                for slot, q in pieces
            ],
            axis=0,
        )

    @pl.loop(0, 4)
    def _(i):
        for sub in range(2):
            at = (2 * i + sub) * rows
            ybuf[:, pl.ds(pl.multiple_of(at * LANES, LANES), wide)] = jnp.dot(
                kown[: 3 * cl], slabs_at(at, own_all), preferred_element_type=jnp.float32
            )

    def input_part(first_step, last_step):
        @pl.loop(first_step, last_step)
        def _(i):
            for sub in range(2):
                at = (2 * i + sub) * rows
                to = pl.ds(pl.multiple_of(at * LANES, LANES), wide)
                total = ybuf[:, to]
                if J > 1:
                    total = total + jnp.dot(
                        kother[: 3 * cl], slabs_at(at, other_all),
                        preferred_element_type=jnp.float32,
                    )
                first = pltpu.roll(total[:cl], wide - 1, 1)
                last = pltpu.roll(total[2 * cl :], 1, 1)
                result = total[cl : 2 * cl] + jnp.where(cols == LANES - 1, 0.0, first)
                result = result + jnp.where(cols == 0, 0.0, last)
                ig_ref[:, to] = result.astype(jnp.bfloat16)

    for p in range(1, J):
        got = kbuf.at[peer(p)]
        pltpu.make_async_copy(got, got, k_recv.at[peer(p)]).wait()
    if J > 1:
        kother[...] = taps_of(
            [kbuf[q, dh, slot] for dh in range(3) for slot, q in other_all]
        )

    for part in (1, 0):
        for d in (-1, 1):
            @pl.when(valid(d))
            def _():
                for p in range(1, J):
                    arrived(1 + d, peer(p), part)
        if J > 1:
            weight_terms(other_all, part)
        if part == 1:
            gather_start(early)
    pair_start(late)

    input_part(0, 1)
    reduce_start(late)
    input_part(1, 2)
    share_start(early)
    input_part(2, 3)
    gather_start(late)
    input_part(3, 4)
    share_start(late)
    for p in range(J):
        sib_copy(p).wait_recv()
    blocks = [obuf[q].reshape(2 * keep, LANES) for q in range(J)]
    for dh in range(3):
        for slot in range(3):
            at = (dh * 3 + slot) * fl
            for dw in range(3):
                kg_ref[(2 - slot) * 9 + dh * 3 + dw] = jnp.concatenate(
                    [b[at : at + fl, dw * cl : (dw + 1) * cl] for b in blocks], axis=1
                )

    for first in (0, 1):
        for p in range(1, J):
            filt_copy(p, 1 - first).wait_send()
        for d in (-1, 1):
            @pl.when(valid(d))
            def _():
                space_copy(d, first).wait_send()
    for p in range(1, J):
        k_copy(p).wait_send()
        for d in (-1, 1):
            @pl.when(valid(d))
            def _():
                space_forward(d, p, 1).wait_send()

                @pl.when(far(d))
                def _():
                    filt_forward(d, p).wait_send()

                @pl.when(jnp.logical_not(far(d)))
                def _():
                    space_forward(d, p, 0).wait_send()
    for p in range(J):
        pair_copy(p).wait_send()
        rs_each(p, lambda c: c.wait_send())

        @pl.when(is_owner)
        def _():
            ag_each(p, lambda c: c.wait_send())

        sib_copy(p).wait_send()


def on_device(activations, kernel, preact, upstream):
    S, J = lax.axis_size("space"), lax.axis_size("filt")
    fl, depth, H, W = preact.shape
    cl = activations.shape[0]
    cells = H * W
    volume = S * depth * cells
    scale = 1.0 / float(volume) ** 0.5
    masked = jnp.where(preact > 0, upstream, jnp.zeros_like(upstream)).reshape(fl, cells)
    acts = activations.reshape(cl, cells)
    taps = kernel.transpose(2, 3, 4, 0, 1).reshape(27, fl, J * cl)
    chips = S // 2
    tiles = -(-9 * fl // 16)
    R = 8 * -(-tiles // chips)
    owners = -(-8 * tiles // R)
    keep = R * owners
    dims = (S, J, fl, H, R, owners, scale)
    padded = cells + 2 * W
    dma = pltpu.SemaphoreType.DMA
    vmem = pl.BlockSpec(memory_space=pltpu.VMEM)
    peers = max(J - 1, 1)
    ig, kg = pl.pallas_call(
        functools.partial(kernel_body, dims),
        out_shape=(
            jax.ShapeDtypeStruct((cl, cells), jnp.bfloat16),
            jax.ShapeDtypeStruct((27, fl, J * cl), jnp.float32),
        ),
        in_specs=[vmem] * 3,
        out_specs=(vmem, vmem),
        scratch_shapes=[
            pltpu.VMEM((3, J, fl, padded), jnp.bfloat16),
            pltpu.VMEM((padded, LANES), jnp.bfloat16),
            pltpu.VMEM((J, 3, 3, fl, LANES), jnp.bfloat16),
            pltpu.VMEM((J, 3, 3, fl, LANES), jnp.bfloat16),
            pltpu.VMEM((LANES, 9 * fl), jnp.bfloat16),
            pltpu.VMEM((LANES, 9 * peers * fl), jnp.bfloat16),
            pltpu.VMEM((3 * cl, cells), jnp.float32),
            pltpu.VMEM((J, 2 * keep, LANES), jnp.float32),
            pltpu.VMEM((J, keep, LANES), jnp.float32),
            pltpu.VMEM((J, keep, LANES), jnp.float32),
            pltpu.VMEM((J, chips, R, LANES), jnp.float32),
            pltpu.VMEM((J, R, LANES), jnp.float32),
            pltpu.VMEM((J, 2, owners, R, LANES), jnp.float32),
            dma((3, J, 2)), dma((2, 2)), dma((peers, 2)), dma((2, peers, 2)),
            dma((2, peers)), dma((peers,)), dma((J,)),
            dma((J,)), dma((J,)), dma((J, owners)), dma((J,)), dma((J, chips)), dma((J,)),
            dma((J,)), dma((J,)),
        ],
        compiler_params=pltpu.CompilerParams(
            collective_id=0, has_side_effects=True, vmem_limit_bytes=40 * 2**20
        ),
    )(masked, acts, taps)
    input_grad = ig.reshape(cl, depth, H, W)
    kernel_grad = kg.reshape(3, 3, 3, fl, J * cl).transpose(3, 4, 0, 1, 2)
    return (input_grad, kernel_grad)


def solution(mesh):
    in_specs = (
        P("filt", "space", None, None),
        P("filt", None, None, None, None),
        P("filt", "space", None, None),
        P("filt", "space", None, None),
    )
    out_specs = (P("filt", "space", None, None), P("filt", None, None, None, None))
    return jax.shard_map(
        on_device, mesh=mesh, in_specs=in_specs, out_specs=out_specs, check_vma=False
    )
```

```python
import functools

import jax
import jax.numpy as jnp
from jax import lax
from jax.experimental import pallas as pl
from jax.experimental.pallas import tpu as pltpu
from jax.sharding import PartitionSpec as P

MESH = pl.DeviceIdType.MESH
LANES = 128


def kernel_body(
    dims, m_ref, a_ref, k_ref, ig_ref, kg_ref,
    mbuf, abuf, kpart, kbuf, ktr, gbuf, pbuf, hbuf, rbuf, sbuf, obuf,
    m_recv, sp_send, fl_send, spf_send, flf_send, k_send, k_recv,
    pair_send, pair_recv, rs_send, rs_recv, ag_send, ag_recv, sib_send, sib_recv,
):
    S, J, fl, H, R, owners, scale = dims
    s = lax.axis_index("space")
    j = lax.axis_index("filt")
    core = lax.rem(s, 2)
    chip = s // 2
    chips = S // 2
    sibling = s + 1 - 2 * core
    keep = R * owners
    mine = (chip * owners + chips - 1) // chips
    is_owner = jnp.logical_and(mine < owners, (mine * chips) // owners == chip)
    half = (H // 2) * LANES
    cells = H * LANES
    parts = (pl.ds(LANES, half), pl.ds(LANES + half, cells - half))
    k3 = 3 * J * fl
    cl = a_ref.shape[0]

    def valid(d):
        return s > 0 if d < 0 else s < S - 1

    def far(d):
        return core == (0 if d < 0 else 1)

    def peer(p):
        return lax.rem(j + p, J)

    barrier = pltpu.get_barrier_semaphore()
    for d in (-1, 1):
        @pl.when(valid(d))
        def _():
            pl.semaphore_signal(
                barrier, inc=1, device_id={"space": s + d, "filt": j}, device_id_type=MESH
            )

    @pl.loop(1, chips * J)
    def _(step):
        other = lax.rem(chip * J + j + step, chips * J)
        pl.semaphore_signal(
            barrier, inc=1,
            device_id={"space": 2 * (other // J) + core, "filt": lax.rem(other, J)},
            device_id_type=MESH,
        )

    edge = jnp.zeros((3, J, fl, LANES), jnp.bfloat16)
    mbuf[:, :, :, :LANES] = edge
    mbuf[:, :, :, LANES + cells :] = edge
    mbuf[1, j, :, LANES : LANES + cells] = m_ref[...]

    @pl.when(s == 0)
    def _():
        mbuf[0, :, :, LANES : LANES + cells] = jnp.zeros((J, fl, cells), jnp.bfloat16)

    @pl.when(s == S - 1)
    def _():
        mbuf[2, :, :, LANES : LANES + cells] = jnp.zeros((J, fl, cells), jnp.bfloat16)

    next_to = (s > 0).astype(jnp.int32) + (s < S - 1).astype(jnp.int32)
    pl.semaphore_wait(barrier, chips * J - 1 + next_to)

    def slab_copy(slot, owner, part, to_slot, space, filt, send):
        return pltpu.make_async_remote_copy(
            src_ref=mbuf.at[slot, owner, :, parts[part]],
            dst_ref=mbuf.at[to_slot, owner, :, parts[part]],
            send_sem=send,
            recv_sem=m_recv.at[to_slot, owner, part],
            device_id={"space": space, "filt": filt},
            device_id_type=MESH,
        )

    def arrived(slot, owner, part):
        ref = mbuf.at[slot, owner, :, parts[part]]
        pltpu.make_async_copy(ref, ref, m_recv.at[slot, owner, part]).wait()

    def k_copy(p):
        return pltpu.make_async_remote_copy(
            src_ref=kpart.at[peer(p)], dst_ref=kbuf.at[j],
            send_sem=k_send.at[p - 1], recv_sem=k_recv.at[j],
            device_id={"space": s, "filt": peer(p)}, device_id_type=MESH,
        )

    def space_copy(d, part):
        return slab_copy(1, j, part, 1 - d, s + d, j, sp_send.at[(d + 1) // 2, part])

    def filt_copy(p, part):
        return slab_copy(1, j, part, 1, s, peer(p), fl_send.at[p - 1, part])

    def space_forward(d, p, part):
        return slab_copy(
            1, peer(p), part, 1 - d, s + d, j, spf_send.at[(d + 1) // 2, p - 1, part]
        )

    def filt_forward(d, p):
        return slab_copy(1 + d, j, 0, 1 + d, s, peer(p), flf_send.at[(d + 1) // 2, p - 1])

    for first in (0, 1):
        for p in range(1, J):
            filt_copy(p, 1 - first).start()
        for d in (-1, 1):
            @pl.when(valid(d))
            def _():
                space_copy(d, first).start()

    abuf[:LANES] = jnp.zeros((LANES, LANES), jnp.bfloat16)
    abuf[LANES + cells :] = jnp.zeros((LANES, LANES), jnp.bfloat16)
    gbuf[...] = jnp.zeros_like(gbuf)
    column = lax.broadcasted_iota(jnp.int32, (cl, LANES), 1)

    @pl.loop(0, H)
    def _(row):
        base = pl.multiple_of(row * LANES, LANES)
        x = a_ref[:, pl.ds(base, LANES)].astype(jnp.float32)
        left = jnp.where(column == 0, 0.0, pltpu.roll(x, 1, 1))
        right = jnp.where(column == LANES - 1, 0.0, pltpu.roll(x, LANES - 1, 1))
        rest = jnp.zeros((LANES - 3 * cl, LANES), jnp.float32)
        stacked = jnp.concatenate([left, x, right, rest], axis=0)
        to = pl.ds(pl.multiple_of(row * LANES + LANES, LANES), LANES)
        abuf[to, :] = stacked.T.astype(jnp.bfloat16)

    for q in range(J):
        for dh in range(3):
            for slot in range(3):
                taps = [
                    k_ref[(2 - slot) * 9 + dh * 3 + dw].astype(jnp.float32)[
                        :, q * cl : (q + 1) * cl
                    ]
                    for dw in range(3)
                ]
                taps.append(jnp.zeros((fl, LANES - 3 * cl), jnp.float32))
                kpart[q, dh, slot] = jnp.concatenate(taps, axis=1).astype(jnp.bfloat16)
    for p in range(1, J):
        k_copy(p).start()
    kbuf[j] = kpart[j]

    def weight_terms(pieces, part):
        rows = H // 4

        @pl.loop(2 * part, 2 * part + 2)
        def _(i):
            base = pl.multiple_of(i * rows * LANES, LANES)
            lhs = jnp.concatenate(
                [mbuf[slot, q, :, pl.ds(base + LANES, rows * LANES)] for slot, q in pieces],
                axis=0,
            )
            rhs = jnp.concatenate(
                [abuf[pl.ds(base + dh * LANES, rows * LANES), :] for dh in range(3)], axis=1
            )
            term = jnp.dot(lhs, rhs, preferred_element_type=jnp.float32)
            for dh in range(3):
                for n, (slot, q) in enumerate(pieces):
                    to = slice((dh * 3 + slot) * fl, (dh * 3 + slot + 1) * fl)
                    gbuf[q, to, :] = gbuf[q, to, :] + term[
                        n * fl : (n + 1) * fl, dh * LANES : (dh + 1) * LANES
                    ]

    def pair_copy(p):
        rows_out = pl.ds(pl.multiple_of((1 - core) * keep, 8), keep)
        return pltpu.make_async_remote_copy(
            src_ref=gbuf.at[peer(p), rows_out], dst_ref=pbuf.at[p],
            send_sem=pair_send.at[p], recv_sem=pair_recv.at[p],
            device_id={"space": sibling, "filt": j}, device_id_type=MESH,
        )

    def rs_copy(p, o):
        return pltpu.make_async_remote_copy(
            src_ref=hbuf.at[p, pl.ds(pl.multiple_of(o * R, 8), R)],
            dst_ref=rbuf.at[j, chip],
            send_sem=rs_send.at[p, o], recv_sem=rs_recv.at[j],
            device_id={"space": 2 * ((o * chips) // owners) + core, "filt": peer(p)},
            device_id_type=MESH,
        )

    def rs_each(p, act):
        @pl.loop(0, owners)
        def _(step):
            o = lax.rem(mine + step, owners)
            if p > 0:
                act(rs_copy(p, o))
            else:
                @pl.when((o * chips) // owners != chip)
                def _():
                    act(rs_copy(p, o))

    def ag_copy(p, t):
        return pltpu.make_async_remote_copy(
            src_ref=sbuf.at[p], dst_ref=obuf.at[peer(p), core, mine],
            send_sem=ag_send.at[p, t], recv_sem=ag_recv.at[peer(p)],
            device_id={"space": 2 * t + core, "filt": j}, device_id_type=MESH,
        )

    def ag_each(p, act):
        @pl.loop(1, chips)
        def _(step):
            act(ag_copy(p, lax.rem(chip + step, chips)))

    def sib_copy(p):
        ref = obuf.at[peer(p), core]
        return pltpu.make_async_remote_copy(
            src_ref=ref, dst_ref=ref,
            send_sem=sib_send.at[p], recv_sem=sib_recv.at[peer(p)],
            device_id={"space": sibling, "filt": j}, device_id_type=MESH,
        )

    def pair_start(stage):
        for p in stage:
            pair_copy(p).start()

    def reduce_start(stage):
        for p in stage:
            pair_copy(p).wait_recv()
            own_rows = pl.ds(pl.multiple_of(core * keep, 8), keep)
            hbuf[p] = gbuf[peer(p), own_rows] + pbuf[p]
            rs_each(p, lambda c: c.start())
            if p == 0:
                @pl.when(is_owner)
                def _():
                    pltpu.make_async_copy(
                        hbuf.at[0, pl.ds(pl.multiple_of(mine * R, 8), R)],
                        rbuf.at[j, chip], rs_recv.at[j],
                    ).start()

    def gather_start(stage):
        @pl.when(is_owner)
        def _():
            for p in stage:
                got = rbuf.at[peer(p)]
                pltpu.make_async_copy(got, got, rs_recv.at[peer(p)]).wait()
                total = rbuf[peer(p), 0]
                for t in range(1, chips):
                    total = total + rbuf[peer(p), t]
                sbuf[p] = total * scale
                ag_each(p, lambda c: c.start())
                pltpu.make_async_copy(
                    sbuf.at[p], obuf.at[peer(p), core, mine], ag_recv.at[peer(p)]
                ).start()

    def share_start(stage):
        for p in stage:
            got = obuf.at[peer(p), core]
            pltpu.make_async_copy(got, got, ag_recv.at[peer(p)]).wait()
            sib_copy(p).start()

    early, late = range(0, 1), range(1, J)
    own_all = [(slot, j) for slot in range(3)]
    other_all = [(slot, peer(p)) for p in late for slot in range(3)]

    for p in range(1, J):
        arrived(1, peer(p), 1)
        for d in (-1, 1):
            @pl.when(valid(d))
            def _():
                space_forward(d, p, 1).start()
    for d in (-1, 1):
        @pl.when(valid(d))
        def _():
            arrived(1 + d, j, 0)

            @pl.when(far(d))
            def _():
                for p in range(1, J):
                    filt_forward(d, p).start()
    weight_terms(own_all, 0)
    for p in range(1, J):
        arrived(1, peer(p), 0)
        for d in (-1, 1):
            @pl.when(jnp.logical_and(valid(d), jnp.logical_not(far(d))))
            def _():
                space_forward(d, p, 0).start()
    for d in (-1, 1):
        @pl.when(valid(d))
        def _():
            arrived(1 + d, j, 1)
    weight_terms(own_all, 1)
    pair_start(early)

    for p in range(1, J):
        got = kbuf.at[peer(p)]
        pltpu.make_async_copy(got, got, k_recv.at[peer(p)]).wait()
    stacked = jnp.concatenate(
        [kbuf[q, dh, slot] for dh in range(3) for slot in range(3) for q in range(J)], axis=0
    )
    ktr[...] = stacked.astype(jnp.float32).T.astype(jnp.bfloat16)
    reduce_start(early)

    for part in (1, 0):
        for d in (-1, 1):
            @pl.when(valid(d))
            def _():
                for p in range(1, J):
                    arrived(1 + d, peer(p), part)
        if J > 1:
            weight_terms(other_all, part)
    pair_start(late)

    rows = H // 8
    wide = rows * LANES
    cols = lax.rem(lax.broadcasted_iota(jnp.int32, (cl, wide), 1), LANES)

    def input_part(first_step, last_step):
        @pl.loop(first_step, last_step)
        def _(i):
            for sub in range(2):
                at = (2 * i + sub) * rows
                slabs = [
                    mbuf[
                        :, :, :, pl.ds(pl.multiple_of((at + 2 - dh) * LANES, LANES), wide)
                    ].reshape(k3, wide)
                    for dh in range(3)
                ]
                total = jnp.dot(
                    ktr[: 3 * cl], jnp.concatenate(slabs, axis=0),
                    preferred_element_type=jnp.float32,
                )
                first = pltpu.roll(total[:cl], wide - 1, 1)
                last = pltpu.roll(total[2 * cl :], 1, 1)
                result = total[cl : 2 * cl] + jnp.where(cols == LANES - 1, 0.0, first)
                result = result + jnp.where(cols == 0, 0.0, last)
                to = pl.ds(pl.multiple_of(at * LANES, LANES), wide)
                ig_ref[:, to] = result.astype(jnp.bfloat16)

    gather_start(early)
    input_part(0, 1)
    reduce_start(late)
    input_part(1, 3)
    gather_start(late)
    share_start(early)
    input_part(3, 4)
    share_start(late)
    for p in range(J):
        sib_copy(p).wait_recv()
    blocks = [obuf[q].reshape(2 * keep, LANES) for q in range(J)]
    for dh in range(3):
        for slot in range(3):
            at = (dh * 3 + slot) * fl
            for dw in range(3):
                kg_ref[(2 - slot) * 9 + dh * 3 + dw] = jnp.concatenate(
                    [b[at : at + fl, dw * cl : (dw + 1) * cl] for b in blocks], axis=1
                )

    for first in (0, 1):
        for p in range(1, J):
            filt_copy(p, 1 - first).wait_send()
        for d in (-1, 1):
            @pl.when(valid(d))
            def _():
                space_copy(d, first).wait_send()
    for p in range(1, J):
        k_copy(p).wait_send()
        for d in (-1, 1):
            @pl.when(valid(d))
            def _():
                space_forward(d, p, 1).wait_send()

                @pl.when(far(d))
                def _():
                    filt_forward(d, p).wait_send()

                @pl.when(jnp.logical_not(far(d)))
                def _():
                    space_forward(d, p, 0).wait_send()
    for p in range(J):
        pair_copy(p).wait_send()
        rs_each(p, lambda c: c.wait_send())

        @pl.when(is_owner)
        def _():
            ag_each(p, lambda c: c.wait_send())

        sib_copy(p).wait_send()


def on_device(activations, kernel, preact, upstream):
    S, J = lax.axis_size("space"), lax.axis_size("filt")
    fl, depth, H, W = preact.shape
    cl = activations.shape[0]
    cells = H * W
    volume = S * depth * cells
    scale = 1.0 / float(volume) ** 0.5
    masked = jnp.where(preact > 0, upstream, jnp.zeros_like(upstream)).reshape(fl, cells)
    acts = activations.reshape(cl, cells)
    taps = kernel.transpose(2, 3, 4, 0, 1).reshape(27, fl, J * cl)
    chips = S // 2
    tiles = -(-9 * fl // 16)
    R = 8 * -(-tiles // chips)
    owners = -(-8 * tiles // R)
    keep = R * owners
    dims = (S, J, fl, H, R, owners, scale)
    padded = cells + 2 * W
    dma = pltpu.SemaphoreType.DMA
    vmem = pl.BlockSpec(memory_space=pltpu.VMEM)
    peers = max(J - 1, 1)
    ig, kg = pl.pallas_call(
        functools.partial(kernel_body, dims),
        out_shape=(
            jax.ShapeDtypeStruct((cl, cells), jnp.bfloat16),
            jax.ShapeDtypeStruct((27, fl, J * cl), jnp.float32),
        ),
        in_specs=[vmem] * 3,
        out_specs=(vmem, vmem),
        scratch_shapes=[
            pltpu.VMEM((3, J, fl, padded), jnp.bfloat16),
            pltpu.VMEM((padded, LANES), jnp.bfloat16),
            pltpu.VMEM((J, 3, 3, fl, LANES), jnp.bfloat16),
            pltpu.VMEM((J, 3, 3, fl, LANES), jnp.bfloat16),
            pltpu.VMEM((LANES, 9 * J * fl), jnp.bfloat16),
            pltpu.VMEM((J, 2 * keep, LANES), jnp.float32),
            pltpu.VMEM((J, keep, LANES), jnp.float32),
            pltpu.VMEM((J, keep, LANES), jnp.float32),
            pltpu.VMEM((J, chips, R, LANES), jnp.float32),
            pltpu.VMEM((J, R, LANES), jnp.float32),
            pltpu.VMEM((J, 2, owners, R, LANES), jnp.float32),
            dma((3, J, 2)), dma((2, 2)), dma((peers, 2)), dma((2, peers, 2)),
            dma((2, peers)), dma((peers,)), dma((J,)),
            dma((J,)), dma((J,)), dma((J, owners)), dma((J,)), dma((J, chips)), dma((J,)),
            dma((J,)), dma((J,)),
        ],
        compiler_params=pltpu.CompilerParams(
            collective_id=0, has_side_effects=True, vmem_limit_bytes=40 * 2**20
        ),
    )(masked, acts, taps)
    input_grad = ig.reshape(cl, depth, H, W)
    kernel_grad = kg.reshape(3, 3, 3, fl, J * cl).transpose(3, 4, 0, 1, 2)
    return (input_grad, kernel_grad)


def solution(mesh):
    in_specs = (
        P("filt", "space", None, None),
        P("filt", None, None, None, None),
        P("filt", "space", None, None),
        P("filt", "space", None, None),
    )
    out_specs = (P("filt", "space", None, None), P("filt", None, None, None, None))
    return jax.shard_map(
        on_device, mesh=mesh, in_specs=in_specs, out_specs=out_specs, check_vma=False
    )
```

```python
import functools

import jax
import jax.numpy as jnp
from jax import lax
from jax.experimental import pallas as pl
from jax.experimental.pallas import tpu as pltpu
from jax.sharding import PartitionSpec as P

MESH = pl.DeviceIdType.MESH
LANES = 128


def kernel_body(
    dims, m_ref, a_ref, k_ref, ig_ref, kg_ref,
    kraw, mbuf, abuf, kpart, kbuf, ktr, gbuf, pbuf, hbuf, rbuf, sbuf, obuf,
    k_in, m_recv, sp_send, fl_send, spf_send, flf_send, k_send, k_recv,
    pair_send, pair_recv, rs_send, rs_recv, ag_send, ag_recv, sib_send, sib_recv,
):
    S, J, fl, H, R, owners, scale = dims
    s = lax.axis_index("space")
    j = lax.axis_index("filt")
    core = lax.rem(s, 2)
    chip = s // 2
    chips = S // 2
    sibling = s + 1 - 2 * core
    keep = R * owners
    mine = (chip * owners + chips - 1) // chips
    is_owner = jnp.logical_and(mine < owners, (mine * chips) // owners == chip)
    half = (H // 2) * LANES
    cells = H * LANES
    parts = (pl.ds(LANES, half), pl.ds(LANES + half, cells - half))
    k3 = 3 * J * fl
    cl = a_ref.shape[0]

    def valid(d):
        return s > 0 if d < 0 else s < S - 1

    def far(d):
        return core == (0 if d < 0 else 1)

    def peer(p):
        return lax.rem(j + p, J)

    load = pltpu.make_async_copy(k_ref, kraw, k_in)
    load.start()
    barrier = pltpu.get_barrier_semaphore()
    for d in (-1, 1):
        @pl.when(valid(d))
        def _():
            pl.semaphore_signal(
                barrier, inc=1, device_id={"space": s + d, "filt": j}, device_id_type=MESH
            )

    @pl.loop(1, chips * J)
    def _(step):
        other = lax.rem(chip * J + j + step, chips * J)
        pl.semaphore_signal(
            barrier, inc=1,
            device_id={"space": 2 * (other // J) + core, "filt": lax.rem(other, J)},
            device_id_type=MESH,
        )

    edge = jnp.zeros((3, J, fl, LANES), jnp.bfloat16)
    mbuf[:, :, :, :LANES] = edge
    mbuf[:, :, :, LANES + cells :] = edge
    mbuf[1, j, :, LANES : LANES + cells] = m_ref[...]

    @pl.when(s == 0)
    def _():
        mbuf[0, :, :, LANES : LANES + cells] = jnp.zeros((J, fl, cells), jnp.bfloat16)

    @pl.when(s == S - 1)
    def _():
        mbuf[2, :, :, LANES : LANES + cells] = jnp.zeros((J, fl, cells), jnp.bfloat16)

    next_to = (s > 0).astype(jnp.int32) + (s < S - 1).astype(jnp.int32)
    pl.semaphore_wait(barrier, chips * J - 1 + next_to)

    def slab_copy(slot, owner, part, to_slot, space, filt, send):
        return pltpu.make_async_remote_copy(
            src_ref=mbuf.at[slot, owner, :, parts[part]],
            dst_ref=mbuf.at[to_slot, owner, :, parts[part]],
            send_sem=send,
            recv_sem=m_recv.at[to_slot, owner, part],
            device_id={"space": space, "filt": filt},
            device_id_type=MESH,
        )

    def arrived(slot, owner, part):
        ref = mbuf.at[slot, owner, :, parts[part]]
        pltpu.make_async_copy(ref, ref, m_recv.at[slot, owner, part]).wait()

    def k_copy(p):
        return pltpu.make_async_remote_copy(
            src_ref=kpart.at[peer(p)], dst_ref=kbuf.at[j],
            send_sem=k_send.at[p - 1], recv_sem=k_recv.at[j],
            device_id={"space": s, "filt": peer(p)}, device_id_type=MESH,
        )

    def space_copy(d, part):
        return slab_copy(1, j, part, 1 - d, s + d, j, sp_send.at[(d + 1) // 2, part])

    def filt_copy(p, part):
        return slab_copy(1, j, part, 1, s, peer(p), fl_send.at[p - 1, part])

    def space_forward(d, p, part):
        return slab_copy(
            1, peer(p), part, 1 - d, s + d, j, spf_send.at[(d + 1) // 2, p - 1, part]
        )

    def filt_forward(d, p):
        return slab_copy(1 + d, j, 0, 1 + d, s, peer(p), flf_send.at[(d + 1) // 2, p - 1])

    for first in (0, 1):
        for p in range(1, J):
            filt_copy(p, 1 - first).start()
        for d in (-1, 1):
            @pl.when(valid(d))
            def _():
                space_copy(d, first).start()

    abuf[:LANES] = jnp.zeros((LANES, LANES), jnp.bfloat16)
    abuf[LANES + cells :] = jnp.zeros((LANES, LANES), jnp.bfloat16)
    gbuf[...] = jnp.zeros_like(gbuf)
    column = lax.broadcasted_iota(jnp.int32, (cl, LANES), 1)

    @pl.loop(0, H)
    def _(row):
        base = pl.multiple_of(row * LANES, LANES)
        x = a_ref[:, pl.ds(base, LANES)].astype(jnp.float32)
        left = jnp.where(column == 0, 0.0, pltpu.roll(x, 1, 1))
        right = jnp.where(column == LANES - 1, 0.0, pltpu.roll(x, LANES - 1, 1))
        rest = jnp.zeros((LANES - 3 * cl, LANES), jnp.float32)
        stacked = jnp.concatenate([left, x, right, rest], axis=0)
        to = pl.ds(pl.multiple_of(row * LANES + LANES, LANES), LANES)
        abuf[to, :] = stacked.T.astype(jnp.bfloat16)

    load.wait()

    for q in range(J):
        for dh in range(3):
            for slot in range(3):
                taps = [
                    kraw[(2 - slot) * 9 + dh * 3 + dw].astype(jnp.float32)[
                        :, q * cl : (q + 1) * cl
                    ]
                    for dw in range(3)
                ]
                taps.append(jnp.zeros((fl, LANES - 3 * cl), jnp.float32))
                kpart[q, dh, slot] = jnp.concatenate(taps, axis=1).astype(jnp.bfloat16)
    for p in range(1, J):
        k_copy(p).start()
    kbuf[j] = kpart[j]

    def weight_terms(pieces, part):
        rows = H // 4

        @pl.loop(2 * part, 2 * part + 2)
        def _(i):
            base = pl.multiple_of(i * rows * LANES, LANES)
            lhs = jnp.concatenate(
                [mbuf[slot, q, :, pl.ds(base + LANES, rows * LANES)] for slot, q in pieces],
                axis=0,
            )
            rhs = jnp.concatenate(
                [abuf[pl.ds(base + dh * LANES, rows * LANES), :] for dh in range(3)], axis=1
            )
            term = jnp.dot(lhs, rhs, preferred_element_type=jnp.float32)
            for dh in range(3):
                for n, (slot, q) in enumerate(pieces):
                    to = slice((dh * 3 + slot) * fl, (dh * 3 + slot + 1) * fl)
                    gbuf[q, to, :] = gbuf[q, to, :] + term[
                        n * fl : (n + 1) * fl, dh * LANES : (dh + 1) * LANES
                    ]

    def pair_copy(p):
        rows_out = pl.ds(pl.multiple_of((1 - core) * keep, 8), keep)
        return pltpu.make_async_remote_copy(
            src_ref=gbuf.at[peer(p), rows_out], dst_ref=pbuf.at[p],
            send_sem=pair_send.at[p], recv_sem=pair_recv.at[p],
            device_id={"space": sibling, "filt": j}, device_id_type=MESH,
        )

    def rs_copy(p, o):
        return pltpu.make_async_remote_copy(
            src_ref=hbuf.at[p, pl.ds(pl.multiple_of(o * R, 8), R)],
            dst_ref=rbuf.at[j, chip],
            send_sem=rs_send.at[p, o], recv_sem=rs_recv.at[j],
            device_id={"space": 2 * ((o * chips) // owners) + core, "filt": peer(p)},
            device_id_type=MESH,
        )

    def rs_each(p, act):
        @pl.loop(0, owners)
        def _(step):
            o = lax.rem(mine + step, owners)
            if p > 0:
                act(rs_copy(p, o))
            else:
                @pl.when((o * chips) // owners != chip)
                def _():
                    act(rs_copy(p, o))

    def ag_copy(p, t):
        return pltpu.make_async_remote_copy(
            src_ref=sbuf.at[p], dst_ref=obuf.at[peer(p), core, mine],
            send_sem=ag_send.at[p, t], recv_sem=ag_recv.at[peer(p)],
            device_id={"space": 2 * t + core, "filt": j}, device_id_type=MESH,
        )

    def ag_each(p, act):
        @pl.loop(1, chips)
        def _(step):
            act(ag_copy(p, lax.rem(chip + step, chips)))

    def sib_copy(p):
        ref = obuf.at[peer(p), core]
        return pltpu.make_async_remote_copy(
            src_ref=ref, dst_ref=ref,
            send_sem=sib_send.at[p], recv_sem=sib_recv.at[peer(p)],
            device_id={"space": sibling, "filt": j}, device_id_type=MESH,
        )

    def pair_start(stage):
        for p in stage:
            pair_copy(p).start()

    def reduce_start(stage):
        for p in stage:
            pair_copy(p).wait_recv()
            own_rows = pl.ds(pl.multiple_of(core * keep, 8), keep)
            hbuf[p] = gbuf[peer(p), own_rows] + pbuf[p]
            rs_each(p, lambda c: c.start())
            if p == 0:
                @pl.when(is_owner)
                def _():
                    pltpu.make_async_copy(
                        hbuf.at[0, pl.ds(pl.multiple_of(mine * R, 8), R)],
                        rbuf.at[j, chip], rs_recv.at[j],
                    ).start()

    def gather_start(stage):
        @pl.when(is_owner)
        def _():
            for p in stage:
                got = rbuf.at[peer(p)]
                pltpu.make_async_copy(got, got, rs_recv.at[peer(p)]).wait()
                total = rbuf[peer(p), 0]
                for t in range(1, chips):
                    total = total + rbuf[peer(p), t]
                sbuf[p] = total * scale
                ag_each(p, lambda c: c.start())
                pltpu.make_async_copy(
                    sbuf.at[p], obuf.at[peer(p), core, mine], ag_recv.at[peer(p)]
                ).start()

    def share_start(stage):
        for p in stage:
            got = obuf.at[peer(p), core]
            pltpu.make_async_copy(got, got, ag_recv.at[peer(p)]).wait()
            sib_copy(p).start()

    early, late = range(0, 1), range(1, J)
    own_all = [(slot, j) for slot in range(3)]
    other_all = [(slot, peer(p)) for p in late for slot in range(3)]

    for p in range(1, J):
        arrived(1, peer(p), 1)
        for d in (-1, 1):
            @pl.when(valid(d))
            def _():
                space_forward(d, p, 1).start()
    for d in (-1, 1):
        @pl.when(valid(d))
        def _():
            arrived(1 + d, j, 0)

            @pl.when(far(d))
            def _():
                for p in range(1, J):
                    filt_forward(d, p).start()
    weight_terms(own_all, 0)
    for p in range(1, J):
        arrived(1, peer(p), 0)
        for d in (-1, 1):
            @pl.when(jnp.logical_and(valid(d), jnp.logical_not(far(d))))
            def _():
                space_forward(d, p, 0).start()
    for d in (-1, 1):
        @pl.when(valid(d))
        def _():
            arrived(1 + d, j, 1)
    weight_terms(own_all, 1)
    pair_start(early)

    for p in range(1, J):
        got = kbuf.at[peer(p)]
        pltpu.make_async_copy(got, got, k_recv.at[peer(p)]).wait()
    stacked = jnp.concatenate(
        [kbuf[q, dh, slot] for dh in range(3) for slot in range(3) for q in range(J)], axis=0
    )
    ktr[...] = stacked.astype(jnp.float32).T.astype(jnp.bfloat16)
    reduce_start(early)

    for part in (1, 0):
        for d in (-1, 1):
            @pl.when(valid(d))
            def _():
                for p in range(1, J):
                    arrived(1 + d, peer(p), part)
        if J > 1:
            weight_terms(other_all, part)
    pair_start(late)

    rows = H // 8
    wide = rows * LANES
    cols = lax.rem(lax.broadcasted_iota(jnp.int32, (cl, wide), 1), LANES)

    def input_part(first_step, last_step):
        @pl.loop(first_step, last_step)
        def _(i):
            for sub in range(2):
                at = (2 * i + sub) * rows
                slabs = [
                    mbuf[
                        :, :, :, pl.ds(pl.multiple_of((at + 2 - dh) * LANES, LANES), wide)
                    ].reshape(k3, wide)
                    for dh in range(3)
                ]
                total = jnp.dot(
                    ktr[: 3 * cl], jnp.concatenate(slabs, axis=0),
                    preferred_element_type=jnp.float32,
                )
                first = pltpu.roll(total[:cl], wide - 1, 1)
                last = pltpu.roll(total[2 * cl :], 1, 1)
                result = total[cl : 2 * cl] + jnp.where(cols == LANES - 1, 0.0, first)
                result = result + jnp.where(cols == 0, 0.0, last)
                to = pl.ds(pl.multiple_of(at * LANES, LANES), wide)
                ig_ref[:, to] = result.astype(jnp.bfloat16)

    gather_start(early)
    input_part(0, 1)
    reduce_start(late)
    input_part(1, 3)
    gather_start(late)
    share_start(early)
    input_part(3, 4)
    share_start(late)
    for p in range(J):
        sib_copy(p).wait_recv()
    blocks = [obuf[q].reshape(2 * keep, LANES) for q in range(J)]
    for dh in range(3):
        for slot in range(3):
            at = (dh * 3 + slot) * fl
            for dw in range(3):
                kg_ref[(2 - slot) * 9 + dh * 3 + dw] = jnp.concatenate(
                    [b[at : at + fl, dw * cl : (dw + 1) * cl] for b in blocks], axis=1
                )

    for first in (0, 1):
        for p in range(1, J):
            filt_copy(p, 1 - first).wait_send()
        for d in (-1, 1):
            @pl.when(valid(d))
            def _():
                space_copy(d, first).wait_send()
    for p in range(1, J):
        k_copy(p).wait_send()
        for d in (-1, 1):
            @pl.when(valid(d))
            def _():
                space_forward(d, p, 1).wait_send()

                @pl.when(far(d))
                def _():
                    filt_forward(d, p).wait_send()

                @pl.when(jnp.logical_not(far(d)))
                def _():
                    space_forward(d, p, 0).wait_send()
    for p in range(J):
        pair_copy(p).wait_send()
        rs_each(p, lambda c: c.wait_send())

        @pl.when(is_owner)
        def _():
            ag_each(p, lambda c: c.wait_send())

        sib_copy(p).wait_send()


def on_device(activations, kernel, preact, upstream):
    S, J = lax.axis_size("space"), lax.axis_size("filt")
    fl, depth, H, W = preact.shape
    cl = activations.shape[0]
    cells = H * W
    volume = S * depth * cells
    scale = 1.0 / float(volume) ** 0.5
    masked = jnp.where(preact > 0, upstream, jnp.zeros_like(upstream)).reshape(fl, cells)
    acts = activations.reshape(cl, cells)
    taps = kernel.transpose(2, 3, 4, 0, 1).reshape(27, fl, J * cl)
    chips = S // 2
    tiles = -(-9 * fl // 16)
    R = 8 * -(-tiles // chips)
    owners = -(-8 * tiles // R)
    keep = R * owners
    dims = (S, J, fl, H, R, owners, scale)
    padded = cells + 2 * W
    dma = pltpu.SemaphoreType.DMA
    vmem = pl.BlockSpec(memory_space=pltpu.VMEM)
    peers = max(J - 1, 1)
    ig, kg = pl.pallas_call(
        functools.partial(kernel_body, dims),
        out_shape=(
            jax.ShapeDtypeStruct((cl, cells), jnp.bfloat16),
            jax.ShapeDtypeStruct((27, fl, J * cl), jnp.float32),
        ),
        in_specs=[vmem, vmem, pl.BlockSpec(memory_space=pltpu.HBM)],
        out_specs=(vmem, vmem),
        scratch_shapes=[
            pltpu.VMEM((27, fl, J * cl), jnp.bfloat16),
            pltpu.VMEM((3, J, fl, padded), jnp.bfloat16),
            pltpu.VMEM((padded, LANES), jnp.bfloat16),
            pltpu.VMEM((J, 3, 3, fl, LANES), jnp.bfloat16),
            pltpu.VMEM((J, 3, 3, fl, LANES), jnp.bfloat16),
            pltpu.VMEM((LANES, 9 * J * fl), jnp.bfloat16),
            pltpu.VMEM((J, 2 * keep, LANES), jnp.float32),
            pltpu.VMEM((J, keep, LANES), jnp.float32),
            pltpu.VMEM((J, keep, LANES), jnp.float32),
            pltpu.VMEM((J, chips, R, LANES), jnp.float32),
            pltpu.VMEM((J, R, LANES), jnp.float32),
            pltpu.VMEM((J, 2, owners, R, LANES), jnp.float32),
            dma, dma((3, J, 2)), dma((2, 2)), dma((peers, 2)), dma((2, peers, 2)),
            dma((2, peers)), dma((peers,)), dma((J,)),
            dma((J,)), dma((J,)), dma((J, owners)), dma((J,)), dma((J, chips)), dma((J,)),
            dma((J,)), dma((J,)),
        ],
        compiler_params=pltpu.CompilerParams(
            collective_id=0, has_side_effects=True, vmem_limit_bytes=62 * 2**20
        ),
    )(masked, acts, taps)
    input_grad = ig.reshape(cl, depth, H, W)
    kernel_grad = kg.reshape(3, 3, 3, fl, J * cl).transpose(3, 4, 0, 1, 2)
    return (input_grad, kernel_grad)


def solution(mesh):
    in_specs = (
        P("filt", "space", None, None),
        P("filt", None, None, None, None),
        P("filt", "space", None, None),
        P("filt", "space", None, None),
    )
    out_specs = (P("filt", "space", None, None), P("filt", None, None, None, None))
    return jax.shard_map(
        on_device, mesh=mesh, in_specs=in_specs, out_specs=out_specs, check_vma=False
    )
```
